32 devices in a mesh: rep: 8 (over z, core), shard: 4 (over y, x).
Axes of the slice: x: 2, y: 2, z: 4, core: 2. Of those that a mesh axis runs over, the one named last changes fastest.
Arguments:
- tokens: bfloat16 [8, 1024, 2048], P('rep', 'shard'), may hold values from -8 to 8
- piece_start: int32 [8], P('rep'), may hold values from 0 to 768
- positions: int32 [8, 1024], P('rep', 'shard'), may hold values from 0 to 2046, as said below
- w_query: float32 [2048, 2048], P('shard', 'rep'), may hold values from -0.125 to 0.125
- w_key: float32 [2048, 2048], P('shard', 'rep'), may hold values from -0.125 to 0.125
- w_value: float32 [2048, 2048], P('shard', 'rep'), may hold values from -0.125 to 0.125
- w_out: float32 [2048, 2048], P('shard', 'rep'), may hold values from -0.125 to 0.125
- query_gain: float32 [2048], P('shard'), may hold values from 0.9 to 1.6
- key_gain: float32 [2048], P('shard'), may hold values from 0.9 to 1.6
- attn_gain: float32 [2048], P('shard'), may hold values from 0.5 to 1.5
- w_gate: float32 [2048, 8192], P('shard', 'rep'), may hold values from -0.125 to 0.125
- w_up: float32 [2048, 8192], P('shard', 'rep'), may hold values from -0.125 to 0.125
- w_down: float32 [8192, 2048], P('shard', 'rep'), may hold values from -0.0625 to 0.0625
- mlp_gain: float32 [2048], P('shard'), may hold values from 0.5 to 1.5
- cotangent: bfloat16 [8, 1024, 2048], P('rep', 'shard'), may hold values from -6 to 6
Outputs:
- output: bfloat16 [8, 1024, 2048], P('rep', 'shard')
- grad_tokens: float32 [8, 1024, 2048], P('rep', 'shard')
- grad_w_query: float32 [2048, 2048], P('shard', 'rep')
- grad_w_key: float32 [2048, 2048], P('shard', 'rep')
- grad_w_value: float32 [2048, 2048], P('shard', 'rep')
- grad_w_out: float32 [2048, 2048], P('shard', 'rep')
- grad_query_gain: float32 [2048], P('shard')
- grad_key_gain: float32 [2048], P('shard')
- grad_attn_gain: float32 [2048], P('shard')
- grad_w_gate: float32 [2048, 8192], P('shard', 'rep')
- grad_w_up: float32 [2048, 8192], P('shard', 'rep')
- grad_w_down: float32 [8192, 2048], P('shard', 'rep')
- grad_mlp_gain: float32 [2048], P('shard')
The draws below stay inside these ranges and needn't reach their ends.
Inputs may be any that keep to these rules, and one draw needn't show every extreme that they name: `positions`: along each sequence the position ids rise by 1 or 2 from one token to the next, and the last token's id is 2046.
All inputs are finite; a program needn't handle non-finite values.
Results may differ from the reference program's by a relative error of at most 0.025.
Values may be sent and summed in bfloat16 or wider, within the bound.
No kernel may reach another device: no remote copies, remote signals or barrier semaphores. Data moves between devices by JAX's collectives and lax.ppermute only.
A program may use at most 512 MiB of HBM per device.

```python
import jax
import jax.numpy as jnp
from jax import lax

D = 2048
HEADS = 16
HEAD_DIM = 128
FF = 8192
SEQ_LEN = 1024
PIECE = 256
SEQS = 8


def draw_tokens(key, part):
    key_scale, key_base = jax.random.split(key, 2)
    row_scale = jnp.exp(jax.random.uniform(key_scale, (SEQS, SEQ_LEN, 1), jnp.float32, -1.15, 1.15))
    values_out = jax.random.normal(key_base, (SEQS, SEQ_LEN, D), jnp.float32) * row_scale
    return jnp.clip(values_out, -8.0, 8.0).astype(jnp.bfloat16)


def draw_positions(key, part):
    key = jax.random.fold_in(key, 7)
    step_ids = jax.random.randint(key, (SEQS, SEQ_LEN - 1), 1, 3, jnp.int32)
    rising = jnp.cumsum(step_ids, axis=1).astype(jnp.int32)
    first_ids = 2 * SEQ_LEN - 2 - rising[:, -1:]
    return jnp.concatenate([first_ids, first_ids + rising], axis=1).astype(jnp.int32)


def with_ends(values, own_key, least, largest):
    place = [jax.random.randint(jax.random.fold_in(own_key, axis), (), 0, length) for axis, length in enumerate(values.shape)]
    main_axis = values.shape.index(max(values.shape))
    beside = place[:main_axis] + [(place[main_axis] + 1) % values.shape[main_axis]] + place[main_axis + 1:]
    return values.at[tuple(place)].set(least).at[tuple(beside)].set(largest)


def block_scale(rng, extent, cuts, low, high):
    loudness, own = 1.0, jax.random.fold_in(rng, 6)
    for position, shards_of in cuts:
        steps = jnp.exp(jax.random.uniform(jax.random.fold_in(own, position), (shards_of,), jnp.float32, low / len(cuts), high / len(cuts)))
        loudness = loudness * jnp.repeat(steps, extent[position] // shards_of).reshape([-1 if axis == position else 1 for axis in range(len(extent))])
    return loudness


def scatter_about(own_key, shape, spread, bound, cuts=(), held_as=jnp.bfloat16):
    array = spread * jax.random.normal(own_key, shape, jnp.float32)
    if cuts:
        array = array * block_scale(own_key, shape, cuts, -0.22, 0.18)
    return jnp.clip(array, -bound, bound).astype(held_as)


def setup_inputs(seed: int = 0) -> dict:
    key_of = jax.random.split(jax.random.key(seed), 16)
    return {
        "tokens": draw_tokens(jax.random.fold_in(key_of[15], 71), 0),
        "piece_start": with_ends(jax.random.randint(key_of[1], (SEQS,), 0, SEQ_LEN - PIECE + 1), jax.random.fold_in(key_of[1], 1), 0, SEQ_LEN - PIECE).astype(jnp.int32),
        "positions": draw_positions(jax.random.fold_in(key_of[15], 71), 0),
        "w_query": scatter_about(key_of[3], (D, D), D ** -0.5, 0.125, ((0, 4), (1, 8)), jnp.float32),
        "w_key": scatter_about(key_of[4], (D, D), D ** -0.5, 0.125, ((0, 4), (1, 8)), jnp.float32),
        "w_value": scatter_about(key_of[5], (D, D), D ** -0.5, 0.125, ((0, 4), (1, 8)), jnp.float32),
        "w_out": scatter_about(key_of[6], (D, D), D ** -0.5, 0.125, ((0, 4), (1, 8)), jnp.float32),
        "query_gain": jnp.clip(0.9 + 0.70000005 * jax.random.uniform(key_of[7], (D,), jnp.float32) ** block_scale(key_of[7], (D,), ((0, 4),), -0.2, 0.2), 0.9, 1.6),
        "key_gain": jnp.clip(0.9 + 0.70000005 * jax.random.uniform(key_of[8], (D,), jnp.float32) ** block_scale(key_of[8], (D,), ((0, 4),), -0.2, 0.2), 0.9, 1.6),
        "attn_gain": jnp.clip(1.0 + 0.1 * jax.random.normal(key_of[9], (D,), jnp.float32), 0.5, 1.5),
        "w_gate": scatter_about(key_of[10], (D, FF), D ** -0.5, 0.125, ((0, 4), (1, 8)), jnp.float32),
        "w_up": scatter_about(key_of[11], (D, FF), D ** -0.5, 0.125, ((0, 4), (1, 8)), jnp.float32),
        "w_down": scatter_about(key_of[12], (FF, D), FF ** -0.5, 0.0625, ((0, 4), (1, 8)), jnp.float32),
        "mlp_gain": jnp.clip(1.0 + 0.1 * jax.random.normal(key_of[13], (D,), jnp.float32), 0.5, 1.5),
        "cotangent": scatter_about(key_of[14], (SEQS, SEQ_LEN, D), 1.0, 6.0, ((0, 8), (1, 4))),
    }


epsilon = 1e-06
rope_base = 500000.0

@jax.custom_vjp
def low(v):
    return lax.optimization_barrier(v.astype(jnp.bfloat16)).astype(jnp.float32)

@jax.custom_vjp
def low_back(v):
    return v

def low_keep(v):
    return (low(v), None)

def low_pass(kept, grad):
    return (grad,)

def back_keep(v):
    return (v, None)

def back_low(kept, grad):
    return (low(grad),)
low.defvjp(low_keep, low_pass)
low_back.defvjp(back_keep, back_low)

def product(left, right):
    return jnp.dot(left, right, precision=lax.Precision.HIGHEST)

def rms_norm(tensor):
    inv_rms = lax.rsqrt(lax.optimization_barrier(jnp.mean(tensor * tensor, axis=-1, keepdims=True)) + epsilon)
    return tensor * inv_rms

def frequencies():
    return jnp.power(jnp.float32(rope_base), -2.0 * jnp.arange(HEAD_DIM // 2, dtype=jnp.float32) / HEAD_DIM)

def rotate(tensor, cosines, sines):
    row_count = tensor.shape[0]
    split_heads = tensor.reshape(row_count, HEADS, 2, HEAD_DIM // 2)
    first_half = split_heads[:, :, 0]
    second_half = split_heads[:, :, 1]
    new_first = first_half * cosines - second_half * sines
    new_second = second_half * cosines + first_half * sines
    return jnp.stack([new_first, new_second], axis=2).reshape(row_count, HEADS * HEAD_DIM)

def piece_mask(piece_first, row_first, row_count, col_count):
    row_pos = row_first + lax.iota(jnp.int32, row_count)[:, None]
    col_pos = lax.iota(jnp.int32, col_count)[None, :]
    row_inside = (row_pos >= piece_first) & (row_pos < piece_first + PIECE)
    col_inside = (col_pos >= piece_first) & (col_pos < piece_first + PIECE)
    return (col_pos <= row_pos) | row_inside & col_inside

def reference(tokens, piece_start, positions, w_query, w_key, w_value, w_out, query_gain, key_gain, attn_gain, w_gate, w_up, w_down, mlp_gain, cotangent):
    angles = positions.astype(jnp.float32)[:, :, None] * frequencies()
    cosines = jnp.cos(angles)[:, :, None, :]
    sines = jnp.sin(angles)[:, :, None, :]
    score_scale = HEAD_DIM ** (-0.5)

    def layer(inputs, query_m, key_m, value_m, out_m, qgain_m, kgain_m, again_m, gate_m, up_m, down_m, mgain_m):
        query_w = low(query_m)
        key_w = low(key_m)
        value_w = low(value_m)
        out_w = low(out_m)
        qgain_w = low(qgain_m)
        kgain_w = low(kgain_m)
        again_w = low(again_m)
        gate_w = low(gate_m)
        up_w = low(up_m)
        down_w = low(down_m)
        mgain_w = low(mgain_m)

        def one_sequence(packed):
            seq_tokens, seq_cos, seq_sin, piece_first = packed
            query_raw = low_back(product(seq_tokens, query_w))
            key_raw = low_back(product(seq_tokens, key_w))
            queries = low(rotate(rms_norm(query_raw) * qgain_w, seq_cos, seq_sin))
            key_rows = low(rotate(rms_norm(key_raw) * kgain_w, seq_cos, seq_sin))
            value_rows = low(low_back(product(seq_tokens, value_w)))
            query_heads = queries.reshape(SEQ_LEN, HEADS, HEAD_DIM)
            key_heads = key_rows.reshape(SEQ_LEN, HEADS, HEAD_DIM)
            value_heads = value_rows.reshape(SEQ_LEN, HEADS, HEAD_DIM)
            scores = jnp.einsum('qhd,khd->hqk', query_heads, key_heads, precision=lax.Precision.HIGHEST) * score_scale
            scores = low_back(scores)
            allowed = piece_mask(piece_first, 0, SEQ_LEN, SEQ_LEN)
            scores = jnp.where(allowed[None], scores, -1e+30)
            softmax_out = jax.nn.softmax(scores, axis=-1)
            mixed_out = jnp.einsum('hqk,khd->qhd', low(softmax_out), value_heads, precision=lax.Precision.HIGHEST)
            mixed_out = low(low_back(mixed_out.reshape(SEQ_LEN, D)))
            branch = low_back(product(mixed_out, out_w))
            hidden = seq_tokens + rms_norm(branch) * again_w
            hidden_low = low(hidden)
            gate_val = low_back(product(hidden_low, gate_w))
            up_val = low_back(product(hidden_low, up_w))
            inner_act = low(jax.nn.silu(gate_val) * up_val)
            second_branch = low_back(product(inner_act, down_w))
            return hidden + rms_norm(second_branch) * mgain_w
        return lax.map(jax.checkpoint(one_sequence), (inputs, cosines, sines, piece_start))
    inputs = tokens.astype(jnp.float32)
    outputs, pullback = jax.vjp(layer, inputs, w_query, w_key, w_value, w_out, query_gain, key_gain, attn_gain, w_gate, w_up, w_down, mlp_gain)
    grads = pullback(cotangent.astype(jnp.float32))
    return (outputs.astype(jnp.bfloat16), grads[0], grads[1], grads[2], grads[3], grads[4], grads[5], grads[6], grads[7], grads[8], grads[9], grads[10], grads[11])
```

```python
import jax
import jax.numpy as jnp
from jax import lax
from jax.sharding import PartitionSpec as P

HEADS = 16
HEAD_DIM = 128
PIECE = 256
SCALE = HEAD_DIM ** (-0.5)

epsilon = 1e-06
rope_base = 500000.0

F32 = jnp.float32
BF16 = jnp.bfloat16

SQUARE = ((0, 0), (0, 2), (1, 0), (1, 1), (0, 1), (0, 3), (1, 2), (1, 3))


def token_order(count):
    return SQUARE if count == 4 else tuple((0, j) for j in range(count))


def to_low(tensor):
    return tensor.astype(BF16)


def dot(left, right, contract):
    return lax.dot_general(left, right, ((contract[0], contract[1]), ((), ())), preferred_element_type=F32)


def mm(left, right):
    return dot(left, right, ((1,), (0,)))


def mm_first(left, right):
    return dot(left, right, ((0,), (0,)))


def mm_last(left, right):
    return dot(left, right, ((1,), (1,)))


def send_shard(value, k):
    count = lax.axis_size("shard")
    return lax.ppermute(value, "shard", [(s, s ^ k) for s in range(count)])


def gather_tokens(own):
    count = lax.axis_size("shard")
    if count != 4:
        return jnp.concatenate([own] + [send_shard(own, k) for k in range(1, count)])
    half = own.shape[0] // 2
    a0, b0 = own[:half], own[half:]
    a2 = send_shard(a0, 2)
    b1 = send_shard(b0, 1)
    a02 = jnp.concatenate([a0, a2])
    b01 = jnp.concatenate([b0, b1])
    a13 = send_shard(a02, 1)
    b23 = send_shard(b01, 2)
    return jnp.concatenate([a02, b01, a13, b23])


def scatter_tokens(keep, send):
    count = lax.axis_size("shard")
    if count != 4:
        parts = jnp.split(jnp.concatenate([keep, send]), count)
        return parts[0] + sum(send_shard(to_low(parts[k]), k).astype(F32) for k in range(1, count))
    q = keep.shape[0] // 2
    send_low = to_low(send)
    a_in = send_shard(send_low[:q], 1)
    b_in = send_shard(send_low[q:], 2)
    a02 = keep[:q] + a_in.astype(F32)
    b01 = keep[q:] + b_in.astype(F32)
    h = q // 2
    a_last = send_shard(to_low(a02[h:]), 2)
    b_last = send_shard(to_low(b01[h:]), 1)
    return jnp.concatenate([a02[:h] + a_last.astype(F32), b01[:h] + b_last.astype(F32)])


def swap_blocks(rows, k):
    order = token_order(lax.axis_size("shard"))
    step = rows.shape[-1] // len(order)
    index = [order.index((h, j ^ k)) for h, j in order]
    return jnp.concatenate([rows[..., i * step : (i + 1) * step] for i in index], axis=-1)


def sum_rows(rows):
    return rows + sum(swap_blocks(send_shard(rows, k), k) for k in range(1, lax.axis_size("shard")))


def unrelative(blocks, s):
    shape = blocks.shape
    bits = shape[0].bit_length() - 1
    cube = blocks.reshape((2,) * bits + shape[1:])
    for bit in range(bits):
        cube = jnp.where((s >> bit) % 2 == 1, jnp.flip(cube, bits - 1 - bit), cube)
    return cube.reshape(shape)


def exchange_shard(blocks, s):
    relative = unrelative(blocks, s)
    got = jnp.stack([relative[0]] + [send_shard(relative[k], k) for k in range(1, blocks.shape[0])])
    return unrelative(got, s)


def rows_perm(count, heads, k):
    c = count // heads
    return [(s, heads * (s % c) + (s // c + k) % heads) for s in range(count)]


def spread_heads(blocks, s):
    heads, count = blocks.shape[0], lax.axis_size("shard")
    q = s // (count // heads)
    got = [lax.ppermute(pick(blocks, (q + k) % heads), "shard", rows_perm(count, heads, k)) for k in range(heads)]
    return reverse_pick(jnp.stack(got), s % heads)


def collect_heads(blocks, s):
    heads, count = blocks.shape[0], lax.axis_size("shard")
    q = s // (count // heads)
    got = [
        lax.ppermute(pick(blocks, (s - k) % heads), "shard", flip(rows_perm(count, heads, k))) for k in range(heads)
    ]
    return roll_pick(jnp.stack(got), -q)


def ring(value, count):
    return lax.ppermute(value, "rep", [(r, (r + 2) % count) for r in range(count)])


def sibling(value, count):
    return lax.ppermute(value, "rep", [(r, r ^ 1) for r in range(count)])


def gather_pairs(own, count):
    pairs = []
    current = own
    for step in range(count // 2):
        if step:
            current = ring(current, count)
        pairs.append(jnp.concatenate([current, sibling(current, count)]))
    return pairs


def scatter_pairs(parts, count):
    half = parts[0].shape[0] // 2
    total = None
    for step in list(range(1, count // 2)) + [0]:
        part = parts[step]
        mine = part[:half] + sibling(to_low(part[half:]), count).astype(F32)
        total = mine if total is None else ring(to_low(total), count).astype(F32) + mine
    return total


def heads_perm(shard_count, rep_count, per, k):
    group = shard_count // per
    pairs = []
    for r in range(rep_count):
        for s in range(shard_count):
            j = (s % per + k) % per
            target = (r // group * group + s // per, per * (r % group) + j)
            pairs.append((r * shard_count + s, target[0] * shard_count + target[1]))
    return pairs


def down_perm(shard_count, rep_count, k):
    m = rep_count // shard_count
    pairs = []
    for r in range(rep_count):
        for s in range(shard_count):
            target = (m * s + (r % m + k) % m, r // m)
            pairs.append((r * shard_count + s, target[0] * shard_count + target[1]))
    return pairs


def flip(pairs):
    return [(b, a) for a, b in pairs]


def permute(value, pairs):
    return lax.ppermute(value, ("rep", "shard"), pairs)


def pick(values, index):
    return lax.dynamic_index_in_dim(values, index, 0, keepdims=False)


def roll_pick(values, shift):
    n = values.shape[0]
    if n == 1:
        return values
    return lax.dynamic_slice_in_dim(jnp.concatenate([values, values]), shift % n, n, 0)


def reverse_pick(values, base):
    n = values.shape[0]
    if n == 1:
        return values
    return roll_pick(values[::-1], n - 1 - base)


def frequencies():
    return jnp.power(jnp.float32(rope_base), -2.0 * jnp.arange(HEAD_DIM // 2, dtype=F32) / HEAD_DIM)


def rotate(tensor, cosines, sines, direction):
    half = HEAD_DIM // 2
    first, second = tensor[..., :half], tensor[..., half:]
    return jnp.concatenate(
        [first * cosines - direction * second * sines, second * cosines + direction * first * sines], axis=-1
    )


def allowed_pairs(piece_first, place):
    inside = (place >= piece_first) & (place < piece_first + PIECE)
    return (place[None, :] <= place[:, None]) | (inside[:, None] & inside[None, :])


def attend(q, k, v, allowed):
    scores = jnp.einsum("hqd,hkd->hqk", q, k, preferred_element_type=F32) * SCALE
    scores = jnp.where(allowed[None], scores, -1e30)
    row_max = jnp.max(scores, axis=-1, keepdims=True)
    log_total = row_max + jnp.log(jnp.sum(jnp.exp(scores - row_max), axis=-1, keepdims=True))
    weights = to_low(jnp.exp(scores - log_total))
    return to_low(jnp.einsum("hqk,hkd->hqd", weights, v, preferred_element_type=F32)), log_total


def attend_back(q, k, v, grad, log_total, allowed):
    scores = jnp.einsum("hqd,hkd->hqk", q, k, preferred_element_type=F32) * SCALE
    scores = jnp.where(allowed[None], scores, -1e30)
    probs = jnp.exp(scores - log_total)
    grad_probs = jnp.einsum("hqd,hkd->hqk", grad, v, preferred_element_type=F32)
    delta = jnp.sum(probs * grad_probs, axis=-1, keepdims=True)
    grad_scores = to_low(probs * (grad_probs - delta))
    dq = jnp.einsum("hqk,hkd->hqd", grad_scores, k, preferred_element_type=F32) * SCALE
    dk = jnp.einsum("hqk,hqd->hkd", grad_scores, q, preferred_element_type=F32) * SCALE
    dv = jnp.einsum("hqk,hqd->hkd", to_low(probs), grad, preferred_element_type=F32)
    return dq, dk, dv


def heads_first(tensor, heads):
    rows, width = tensor.shape
    return tensor.reshape(rows, heads, width // heads).transpose(1, 0, 2)


def heads_last(tensor):
    heads, rows, width = tensor.shape
    return tensor.transpose(1, 0, 2).reshape(rows, heads * width)


def body(
    tokens,
    piece_start,
    positions,
    w_query,
    w_key,
    w_value,
    w_out,
    query_gain,
    key_gain,
    attn_gain,
    w_gate,
    w_up,
    w_down,
    mlp_gain,
    cotangent,
):
    S = lax.axis_size("shard")
    R = lax.axis_size("rep")
    s = lax.axis_index("shard")
    r = lax.axis_index("rep")
    _, span, width = tokens.shape
    heads = HEADS // S
    per = HEADS // R
    m = R // S
    own_width = width // S
    x_own = tokens.reshape(span, width)

    own_qkv = jnp.concatenate(
        [
            to_low(w).reshape(own_width, per, HEAD_DIM).transpose(1, 0, 2)
            for w in (w_query, w_key, w_value)
        ],
        axis=2,
    )
    got = jnp.stack(
        [permute(pick(own_qkv, (s + k) % per), heads_perm(S, R, per, k)) for k in range(per)]
    )
    got = reverse_pick(got, s % per).reshape(per * own_width, 3 * HEAD_DIM)
    qkv_w = lax.all_gather(got, "rep", axis=0, tiled=True).reshape(heads, width, 3 * HEAD_DIM)
    own_out = spread_heads(to_low(w_out).reshape(heads, HEAD_DIM, -1), s).reshape(own_width, -1)
    out_w = lax.all_gather(own_out, "rep", axis=1, tiled=True)

    gains_own = jnp.stack([to_low(g).astype(F32) for g in (query_gain, key_gain, attn_gain, mlp_gain)])
    small = jnp.concatenate([positions.reshape(span).astype(F32), gains_own.reshape(-1)])
    small_all = [small] + [send_shard(small, k) for k in range(1, S)]
    gains = unrelative(jnp.stack([v[span:].reshape(4, own_width) for v in small_all]), s)
    gains = gains.transpose(1, 0, 2).reshape(4, width)
    head_gains = gains[:2].reshape(2, heads, S, HEAD_DIM)
    head_gains = lax.dynamic_index_in_dim(head_gains, s, 2, keepdims=False)
    qgain, kgain = head_gains[0][:, None, :], head_gains[1][:, None, :]
    again, mgain = gains[2], gains[3]
    order = token_order(S)
    step = S * span // len(order)
    place_pos = jnp.concatenate([small_all[j][h * step : (h + 1) * step] for h, j in order])
    place = jnp.concatenate([(s ^ j) * span + h * step + lax.iota(jnp.int32, step) for h, j in order])
    angles = place_pos[:, None] * frequencies()
    cosines, sines = jnp.cos(angles), jnp.sin(angles)
    allowed = allowed_pairs(piece_start[0], place)

    x_all = gather_tokens(x_own)
    raw = jnp.einsum("tk,qkn->qtn", x_all, qkv_w, preferred_element_type=F32)
    qraw, kraw, vraw = raw[..., :HEAD_DIM], raw[..., HEAD_DIM : 2 * HEAD_DIM], raw[..., 2 * HEAD_DIM :]
    squares = jnp.stack([jnp.sum(qraw * qraw, axis=(0, 2)), jnp.sum(kraw * kraw, axis=(0, 2))])
    inv = lax.rsqrt(sum_rows(squares) / width + epsilon)
    qinv, kinv = inv[0][None, :, None], inv[1][None, :, None]
    qhat, khat = qraw * qinv, kraw * kinv
    q = to_low(rotate(qhat * qgain, cosines, sines, 1.0))
    k = to_low(rotate(khat * kgain, cosines, sines, 1.0))
    v = to_low(vraw)
    o_heads, log_total = attend(q, k, v, allowed)
    o = heads_last(o_heads)
    rows = S * span // 2
    a_send = mm(o[rows:], out_w)
    a_keep = mm(o[:rows], out_w)
    a = scatter_tokens(a_keep, a_send)
    ainv = lax.rsqrt(jnp.mean(a * a, axis=-1, keepdims=True) + epsilon)
    ahat = a * ainv
    h = x_own.astype(F32) + ahat * again
    hb = to_low(h)

    gate_w = lax.all_gather(to_low(w_gate), "shard", axis=0, tiled=True)
    up_w = lax.all_gather(to_low(w_up), "shard", axis=0, tiled=True)
    unit = to_low(w_down).reshape(m, w_down.shape[0] // m, w_down.shape[1])
    got = jnp.stack([permute(pick(unit, (r + k) % m), down_perm(S, R, k)) for k in range(m)])
    got = reverse_pick(got, r % m)
    own_down = jnp.concatenate([got[i] for i in range(m)], axis=1)
    down_w = lax.all_gather(own_down, "shard", axis=1, tiled=True)

    hb_pairs = gather_pairs(hb, R)
    kept = []
    z_parts = []
    for pair in hb_pairs:
        g = mm(pair, gate_w)
        u = mm(pair, up_w)
        sig = jax.nn.sigmoid(g)
        inner = to_low(g * sig * u)
        kept.append((g, u, inner))
        z_parts.append(mm(inner, down_w))
    z = scatter_pairs(z_parts, R)
    zinv = lax.rsqrt(jnp.mean(z * z, axis=-1, keepdims=True) + epsilon)
    zhat = z * zinv
    output = to_low(h + zhat * mgain).reshape(tokens.shape)

    dy = cotangent.reshape(span, width).astype(F32)
    grad_mgain = jnp.sum(dy * zhat, axis=0)
    scaled = dy * mgain
    dz = to_low(zinv * (scaled - zhat * jnp.mean(scaled * zhat, axis=-1, keepdims=True)))
    dz_pairs = gather_pairs(dz, R)
    dh_parts, dgs, dus = [], [], []
    for pair, (g, u, inner) in zip(dz_pairs, kept):
        dm = mm_last(pair, down_w)
        sig = jax.nn.sigmoid(g)
        dg = to_low(dm * u * sig * (1.0 + g * (1.0 - sig)))
        du = to_low(dm * g * sig)
        dgs.append(dg)
        dus.append(du)
        dh_parts.append(mm_last(dg, gate_w) + mm_last(du, up_w))
    dh = dy + scatter_pairs(dh_parts, R)
    hb_all = jnp.concatenate(hb_pairs)
    down_grad = to_low(mm_first(jnp.concatenate([t[2] for t in kept]), jnp.concatenate(dz_pairs)))
    gate_grad = to_low(mm_first(hb_all, jnp.concatenate(dgs)))
    up_grad = to_low(mm_first(hb_all, jnp.concatenate(dus)))
    grad_gate = lax.psum_scatter(gate_grad, "shard", scatter_dimension=0, tiled=True).astype(F32)
    grad_up = lax.psum_scatter(up_grad, "shard", scatter_dimension=0, tiled=True).astype(F32)
    down_share = lax.psum_scatter(down_grad, "shard", scatter_dimension=1, tiled=True)
    slots = down_share.reshape(down_share.shape[0], m, -1).transpose(1, 0, 2)
    back = jnp.stack([permute(pick(slots, (r - k) % m), flip(down_perm(S, R, k))) for k in range(m)])
    grad_down = roll_pick(back, -(r % m)).reshape(w_down.shape).astype(F32)

    grad_again = jnp.sum(dh * ahat, axis=0)
    scaled = dh * again
    da = to_low(ainv * (scaled - ahat * jnp.mean(scaled * ahat, axis=-1, keepdims=True)))
    da_all = gather_tokens(da)
    do = heads_first(to_low(mm_last(da_all, out_w)), heads)
    out_grad = to_low(mm_first(o, da_all))
    dq, dk, dv = attend_back(q, k, v, do, log_total, allowed)
    dq_rot = rotate(dq, cosines, sines, -1.0)
    dk_rot = rotate(dk, cosines, sines, -1.0)
    grad_qgain = jnp.sum(dq_rot * qhat, axis=1)
    grad_kgain = jnp.sum(dk_rot * khat, axis=1)
    qs, ks = dq_rot * qgain, dk_rot * kgain
    means = jnp.stack([jnp.sum(qs * qhat, axis=(0, 2)), jnp.sum(ks * khat, axis=(0, 2))])
    means = sum_rows(means) / width
    dqraw = to_low(qinv * (qs - qhat * means[0][None, :, None]))
    dkraw = to_low(kinv * (ks - khat * means[1][None, :, None]))
    dqkv = jnp.concatenate([dqraw, dkraw, to_low(dv)], axis=2)
    dx_send = jnp.einsum("qtn,qkn->tk", dqkv[:, rows:], qkv_w, preferred_element_type=F32)
    dx_keep = jnp.einsum("qtn,qkn->tk", dqkv[:, :rows], qkv_w, preferred_element_type=F32)
    dx = dh + scatter_tokens(dx_keep, dx_send)
    qkv_grad = to_low(jnp.einsum("tk,qtn->qkn", x_all, dqkv, preferred_element_type=F32))
    qkv_grad = qkv_grad.reshape(heads * width, 3 * HEAD_DIM)

    out_share = lax.psum_scatter(out_grad, "rep", scatter_dimension=1, tiled=True)
    grad_out = collect_heads(out_share.reshape(heads, HEAD_DIM, -1), s).reshape(w_out.shape).astype(F32)
    qkv_share = lax.psum_scatter(qkv_grad, "rep", scatter_dimension=0, tiled=True)
    slots = qkv_share.reshape(per, own_width, 3 * HEAD_DIM)
    back = jnp.stack([permute(pick(slots, (s - k) % per), flip(heads_perm(S, R, per, k))) for k in range(per)])
    back = roll_pick(back, -(s % per)).reshape(per, own_width, 3, HEAD_DIM)
    back = back.transpose(2, 1, 0, 3).reshape(3, own_width, per * HEAD_DIM).astype(F32)

    head_grads = collect_heads(jnp.stack([grad_qgain, grad_kgain], axis=1), s)
    head_grads = head_grads.transpose(1, 0, 2).reshape(2, own_width)
    wide = jnp.stack([grad_again, grad_mgain]).reshape(2, S, own_width).transpose(1, 0, 2)
    wide = jnp.sum(exchange_shard(wide, s), axis=0)
    gain_grads = jnp.concatenate([head_grads, wide])
    step = 1
    while step < R:
        gain_grads = gain_grads + lax.ppermute(gain_grads, "rep", [(i, i ^ step) for i in range(R)])
        step *= 2

    return (
        output,
        dx.reshape(tokens.shape),
        back[0],
        back[1],
        back[2],
        grad_out,
        gain_grads[0],
        gain_grads[1],
        gain_grads[2],
        grad_gate,
        grad_up,
        grad_down,
        gain_grads[3],
    )


def solution(mesh):
    grid = P("shard", "rep")
    rows = P("rep", "shard", None)
    gain = P("shard")
    in_specs = (rows, P("rep"), P("rep", "shard"), grid, grid, grid, grid, gain, gain, gain, grid, grid, grid, gain, rows)
    out_specs = (rows, rows, grid, grid, grid, grid, gain, gain, gain, grid, grid, grid, gain)
    return jax.shard_map(body, mesh=mesh, in_specs=in_specs, out_specs=out_specs, check_vma=False)
```

```python
import jax
import jax.numpy as jnp
from jax import lax
from jax.experimental import pallas as pl
from jax.experimental.pallas import tpu as pltpu
from jax.sharding import PartitionSpec as P

HEADS = 16
HEAD_DIM = 128
PIECE = 256
SCALE = HEAD_DIM ** (-0.5)

LOG2_E = 1.4426950408889634
VMEM = 24 << 20
WIDE_VMEM = 56 << 20

epsilon = 1e-06
rope_base = 500000.0

F32 = jnp.float32
BF16 = jnp.bfloat16

SQUARE = ((0, 0), (0, 2), (1, 0), (1, 1), (0, 1), (0, 3), (1, 2), (1, 3))


def token_order(count):
    return SQUARE if count == 4 else tuple((0, j) for j in range(count))


def to_low(tensor):
    return tensor.astype(BF16)


def dot(left, right, contract):
    return lax.dot_general(left, right, ((contract[0], contract[1]), ((), ())), preferred_element_type=F32)


def mm(left, right):
    return dot(left, right, ((1,), (0,)))


def mm_first(left, right):
    return dot(left, right, ((0,), (0,)))


def mm_last(left, right):
    return dot(left, right, ((1,), (1,)))


def after(value, *others):
    return lax.optimization_barrier((value,) + others)[0]


def send_shard(value, k):
    count = lax.axis_size("shard")
    return lax.ppermute(value, "shard", [(s, s ^ k) for s in range(count)])


def gather_tokens(own, first_hold=(), last_hold=()):
    count = lax.axis_size("shard")
    if count != 4:
        others = [send_shard(own, k) for k in range(1, count)]
        return jnp.concatenate([own] + others), others[0]
    half = own.shape[0] // 2
    a0, b0 = own[:half], own[half:]
    a2 = send_shard(a0, 2)
    b1 = send_shard(b0, 1)
    if first_hold:
        a2, b1 = after(a2, *first_hold), after(b1, *first_hold)
    a02 = jnp.concatenate([a0, a2])
    b01 = jnp.concatenate([b0, b1])
    a13 = send_shard(a02, 1)
    b23 = send_shard(b01, 2)
    if last_hold:
        a13, b23 = after(a13, *last_hold), after(b23, *last_hold)
    return jnp.concatenate([a02, b01, a13, b23]), a2


def scatter_tokens(keep, send, first_hold=(), last_hold=()):
    count = lax.axis_size("shard")
    if count != 4:
        parts = jnp.split(jnp.concatenate([keep, send]), count)
        return parts[0] + sum(send_shard(to_low(parts[k]), k).astype(F32) for k in range(1, count))
    q = keep.shape[0] // 2
    send_low = to_low(send)
    a_in = send_shard(send_low[:q], 1)
    b_in = send_shard(send_low[q:], 2)
    if first_hold:
        a_in, b_in = after(a_in, *first_hold), after(b_in, *first_hold)
    a02 = keep[:q] + a_in.astype(F32)
    b01 = keep[q:] + b_in.astype(F32)
    h = q // 2
    a_last = send_shard(to_low(a02[h:]), 2)
    b_last = send_shard(to_low(b01[h:]), 1)
    if last_hold:
        a_last, b_last = after(a_last, *last_hold), after(b_last, *last_hold)
    return jnp.concatenate([a02[:h] + a_last.astype(F32), b01[:h] + b_last.astype(F32)])


def swap_blocks(rows, k):
    order = token_order(lax.axis_size("shard"))
    step = rows.shape[-1] // len(order)
    index = [order.index((h, j ^ k)) for h, j in order]
    return jnp.concatenate([rows[..., i * step : (i + 1) * step] for i in index], axis=-1)


def sum_rows(rows):
    return rows + sum(swap_blocks(send_shard(rows, k), k) for k in range(1, lax.axis_size("shard")))


def unrelative(blocks, s):
    shape = blocks.shape
    bits = shape[0].bit_length() - 1
    cube = blocks.reshape((2,) * bits + shape[1:])
    for bit in range(bits):
        cube = jnp.where((s >> bit) % 2 == 1, jnp.flip(cube, bits - 1 - bit), cube)
    return cube.reshape(shape)


def exchange_shard(blocks, s):
    relative = unrelative(blocks, s)
    got = jnp.stack([relative[0]] + [send_shard(relative[k], k) for k in range(1, blocks.shape[0])])
    return unrelative(got, s)


def rows_perm(count, heads, k):
    c = count // heads
    return [(s, heads * (s % c) + (s // c + k) % heads) for s in range(count)]


def spread_heads(blocks, s):
    heads, count = blocks.shape[0], lax.axis_size("shard")
    q = s // (count // heads)
    got = [lax.ppermute(pick(blocks, (q + k) % heads), "shard", rows_perm(count, heads, k)) for k in range(heads)]
    return reverse_pick(jnp.stack(got), s % heads)


def collect_heads(blocks, s):
    heads, count = blocks.shape[0], lax.axis_size("shard")
    q = s // (count // heads)
    got = [
        lax.ppermute(pick(blocks, (s - k) % heads), "shard", flip(rows_perm(count, heads, k))) for k in range(heads)
    ]
    return roll_pick(jnp.stack(got), -q)


def ring(value, count):
    return lax.ppermute(value, "rep", [(r, (r + 2) % count) for r in range(count)])


def sibling(value, count):
    return lax.ppermute(value, "rep", [(r, r ^ 1) for r in range(count)])


def gather_pairs(own, count):
    blocks = [own]
    for _ in range(count // 2 - 1):
        blocks.append(ring(blocks[-1], count))
    pairs = []
    for i, block in enumerate(blocks):
        other = sibling(block, count)
        pairs.append((block, after(other, blocks[i + 1]) if i + 1 < len(blocks) else other))
    return pairs


def scatter_pairs(part_of, count, beside=lambda i, low: ()):
    total = low = None
    for i, step in enumerate(list(range(1, count // 2)) + [0]):
        part = part_of(step, low)
        half = part.shape[0] // 2
        mine = part[:half] + sibling(to_low(part[half:]), count).astype(F32)
        if total is None:
            total = mine
        else:
            got = ring(low, count)
            hold = beside(i - 1, low)
            if hold:
                got = after(got, *hold)
            total = got.astype(F32) + mine
        low = to_low(total)
    return total


def heads_perm(shard_count, rep_count, per, k):
    group = shard_count // per
    pairs = []
    for r in range(rep_count):
        for s in range(shard_count):
            j = (s % per + k) % per
            target = (r // group * group + s // per, per * (r % group) + j)
            pairs.append((r * shard_count + s, target[0] * shard_count + target[1]))
    return pairs


def flip_rep(value, d):
    count = lax.axis_size("rep")
    return lax.ppermute(value, "rep", [(i, i ^ d) for i in range(count)])


def sum_rep(value):
    return value + sum(flip_rep(value, d) for d in range(1, lax.axis_size("rep")))


def spread_down(rows, s):
    S, R = lax.axis_size("shard"), lax.axis_size("rep")
    columns = rows.shape[1]
    share = rows.shape[0] // R
    units = rows.reshape(R // S, S, share, columns)
    pieces = [lax.dynamic_index_in_dim(units, s ^ k, 1, keepdims=False) for k in range(S)]
    return [pieces[0]] + [send_shard(pieces[k], k) for k in range(1, S)]


def cross_down(pieces, s, r):
    R = lax.axis_size("rep")
    m = pieces[0].shape[0]
    pieces = jnp.concatenate(pieces)
    blocks = [pick(pieces, (((r ^ d) // m) ^ s) * m + (r ^ d) % m) for d in range(R)]
    return [blocks[0]] + [flip_rep(blocks[d], d) for d in range(1, R)]


def join_down(blocks, r):
    share, columns = blocks[0].shape
    out = jnp.zeros((share, len(blocks) * columns), blocks[0].dtype)
    for d, block in enumerate(blocks):
        out = lax.dynamic_update_slice_in_dim(out, block, (r ^ d) * columns, 1)
    return out


def return_cross(rows, r):
    R = lax.axis_size("rep")
    columns = rows.shape[1] // R
    blocks = [lax.dynamic_slice_in_dim(rows, (r ^ d) * columns, columns, 1) for d in range(R)]
    return [blocks[0]] + [flip_rep(blocks[d], d) for d in range(1, R)]


def return_spread(blocks, s, r):
    S, R = lax.axis_size("shard"), lax.axis_size("rep")
    m = R // S
    share, columns = blocks[0].shape
    pieces = jnp.zeros((R, share, columns), blocks[0].dtype)
    for d, block in enumerate(blocks):
        other = r ^ d
        pieces = lax.dynamic_update_slice_in_dim(pieces, block[None], ((other // m) ^ s) * m + other % m, 0)
    pieces = pieces.reshape(S, m, share, columns)
    return [pieces[0]] + [send_shard(pieces[k], k) for k in range(1, S)]


def place_units(pieces, s):
    m, share, columns = pieces[0].shape
    S = len(pieces)
    units = jnp.zeros((m, S, share, columns), pieces[0].dtype)
    for k, piece in enumerate(pieces):
        units = lax.dynamic_update_slice_in_dim(units, piece[:, None], s ^ k, 1)
    return units.reshape(m * S * share, columns)


def flip(pairs):
    return [(b, a) for a, b in pairs]


def permute(value, pairs):
    return lax.ppermute(value, ("rep", "shard"), pairs)


def pick(values, index):
    return lax.dynamic_index_in_dim(values, index, 0, keepdims=False)


def roll_pick(values, shift):
    n = values.shape[0]
    if n == 1:
        return values
    return lax.dynamic_slice_in_dim(jnp.concatenate([values, values]), shift % n, n, 0)


def reverse_pick(values, base):
    n = values.shape[0]
    if n == 1:
        return values
    return roll_pick(values[::-1], n - 1 - base)


def frequencies():
    return jnp.power(jnp.float32(rope_base), -2.0 * jnp.arange(HEAD_DIM // 2, dtype=F32) / HEAD_DIM)


def bias_of(piece_first, row, col):
    row_in = (row >= piece_first) & (row < piece_first + PIECE)
    col_in = (col >= piece_first) & (col < piece_first + PIECE)
    return jnp.where((col <= row) | (row_in & col_in), 0.0, -1e30).astype(F32)


def attend_kernel(where_ref, q_ref, k_ref, v_ref, row_ref, col_ref, o_ref, bias_ref):
    @pl.when(pl.program_id(1) == 0)
    def _():
        bias_ref[...] = bias_of(where_ref[where_ref.shape[0] - 1], row_ref[...], col_ref[...])

    scores = mm_last(q_ref[0], k_ref[0]) * (SCALE * LOG2_E) + bias_ref[...]
    powers = jnp.exp2(scores - jnp.max(scores, axis=-1, keepdims=True))
    weights = powers * (1.0 / jnp.sum(powers, axis=-1, keepdims=True))
    o_ref[...] = to_low(mm(to_low(weights), v_ref[0]))


def attend(q, k, v, place, where, block=256):
    heads, n, hd = q.shape
    whole = pl.BlockSpec((1, n, hd), lambda b, t, w: (t, 0, 0))
    return pl.pallas_call(
        attend_kernel,
        out_shape=jax.ShapeDtypeStruct((n, heads * hd), BF16),
        grid_spec=pltpu.PrefetchScalarGridSpec(
            num_scalar_prefetch=1,
            grid=(n // block, heads),
            in_specs=[
                pl.BlockSpec((1, block, hd), lambda b, t, w: (t, b, 0)),
                whole,
                whole,
                pl.BlockSpec((block, 1), lambda b, t, w: (b, 0)),
                pl.BlockSpec((1, n), lambda b, t, w: (0, 0)),
            ],
            out_specs=pl.BlockSpec((block, hd), lambda b, t, w: (b, w[t])),
            scratch_shapes=[pltpu.VMEM((block, n), F32)],
        ),
        compiler_params=pltpu.CompilerParams(vmem_limit_bytes=VMEM),
        cost_estimate=pl.CostEstimate(
            flops=4 * heads * n * n * hd, bytes_accessed=8 * heads * n * hd, transcendentals=heads * n * n
        ),
        name="attend",
    )(where, q, k, v, place[:, None], place[None, :])


def attend_back_kernel(where_ref, q_ref, k_ref, v_ref, do_ref, row_ref, col_ref, dq_ref, dk_ref, dv_ref, bias_ref):
    b = pl.program_id(1)

    @pl.when(pl.program_id(0) == 0)
    def _():
        bias_ref[b] = bias_of(where_ref[where_ref.shape[0] - 1], row_ref[...], col_ref[...])

    q, k, v, do = q_ref[0], k_ref[0], v_ref[0], do_ref[...]
    scores = mm_last(k, q) * (SCALE * LOG2_E) + bias_ref[b]
    powers = jnp.exp2(scores - jnp.max(scores, axis=0, keepdims=True))
    probs = powers * (1.0 / jnp.sum(powers, axis=0, keepdims=True))
    grad_probs = mm_last(v, do)
    delta = jnp.sum(probs * grad_probs, axis=0, keepdims=True)
    grad_scores = to_low(probs * (grad_probs - delta))
    dq_ref[0] = mm_first(grad_scores, k) * SCALE
    dk = mm(grad_scores, q) * SCALE
    dv = mm(to_low(probs), do)

    @pl.when(b == 0)
    def _():
        dk_ref[0] = dk
        dv_ref[0] = dv

    @pl.when(b > 0)
    def _():
        dk_ref[0] += dk
        dv_ref[0] += dv


def attend_back(q, k, v, do, place, where, block=512):
    heads, n, hd = q.shape
    one = pl.BlockSpec((1, block, hd), lambda t, b, w: (t, b, 0))
    whole = pl.BlockSpec((1, n, hd), lambda t, b, w: (t, 0, 0))
    return pl.pallas_call(
        attend_back_kernel,
        out_shape=[jax.ShapeDtypeStruct((heads, n, hd), F32)] * 3,
        grid_spec=pltpu.PrefetchScalarGridSpec(
            num_scalar_prefetch=1,
            grid=(heads, n // block),
            in_specs=[
                one,
                whole,
                whole,
                pl.BlockSpec((block, hd), lambda t, b, w: (b, w[t])),
                pl.BlockSpec((1, block), lambda t, b, w: (0, b)),
                pl.BlockSpec((n, 1), lambda t, b, w: (0, 0)),
            ],
            out_specs=[one, whole, whole],
            scratch_shapes=[pltpu.VMEM((n // block, n, block), F32)],
        ),
        compiler_params=pltpu.CompilerParams(vmem_limit_bytes=32 << 20),
        cost_estimate=pl.CostEstimate(
            flops=10 * heads * n * n * hd, bytes_accessed=20 * heads * n * hd, transcendentals=heads * n * n
        ),
        name="attend_back",
    )(where, q, k, v, do, place[None, :], place[:, None])


def squares_kernel(heads, *refs):
    for i in (0, 1):
        part = slice(i * HEAD_DIM, (i + 1) * HEAD_DIM)
        total = sum(jnp.square(raw[:, part]) for raw in refs[:heads])
        refs[heads][i : i + 1, :] = jnp.sum(total.T, axis=0, keepdims=True)


def squares(raws, block=256):
    heads = len(raws)
    n = raws[0].shape[0]
    return pl.pallas_call(
        lambda *refs: squares_kernel(heads, *refs),
        out_shape=jax.ShapeDtypeStruct((2, n), F32),
        grid=(n // block,),
        in_specs=[pl.BlockSpec((block, 3 * HEAD_DIM), lambda b: (b, 0))] * heads,
        out_specs=pl.BlockSpec((2, block), lambda b: (0, b)),
        compiler_params=pltpu.CompilerParams(vmem_limit_bytes=VMEM),
        cost_estimate=pl.CostEstimate(flops=heads * n * 512, bytes_accessed=heads * n * 1536, transcendentals=0),
        name="squares",
    )(*raws)


def inner_products_kernel(dq_ref, q_ref, dk_ref, k_ref, out_ref):
    for i, (d_ref, v_ref) in enumerate(((dq_ref, q_ref), (dk_ref, k_ref))):
        total = sum(d_ref[t] * v_ref[t].astype(F32) for t in range(d_ref.shape[0]))
        out_ref[i : i + 1, :] = jnp.sum(total.T, axis=0, keepdims=True)


def inner_products(dq, q, dk, k, block=256):
    heads, n, hd = q.shape
    part = pl.BlockSpec((heads, block, hd), lambda b: (0, b, 0))
    return pl.pallas_call(
        inner_products_kernel,
        out_shape=jax.ShapeDtypeStruct((2, n), F32),
        grid=(n // block,),
        in_specs=[part] * 4,
        out_specs=pl.BlockSpec((2, block), lambda b: (0, b)),
        compiler_params=pltpu.CompilerParams(vmem_limit_bytes=WIDE_VMEM),
        cost_estimate=pl.CostEstimate(flops=heads * n * 512, bytes_accessed=heads * n * 1536, transcendentals=0),
        name="inner_products",
    )(dq, q, dk, k)


def turn_half(tensor):
    return pltpu.roll(tensor, HEAD_DIM // 2, 1)


def rope_kernel(heads, *refs):
    raws, (inv_ref, gain_ref, turn_ref, q_ref, k_ref, v_ref) = refs[:heads], refs[heads:]
    cosines, sines = turn_ref[:, :HEAD_DIM], turn_ref[:, HEAD_DIM:]
    for t in range(heads):
        for i, out in enumerate((q_ref, k_ref)):
            raw = raws[t][:, i * HEAD_DIM : (i + 1) * HEAD_DIM]
            value = raw * inv_ref[:, i : i + 1] * gain_ref[t, i : i + 1, :]
            out[t] = to_low(value * cosines + turn_half(value) * sines)
        v_ref[t] = to_low(raws[t][:, 2 * HEAD_DIM :])


def rope(raws, inv, gain, turn, block=256):
    heads = len(raws)
    n = raws[0].shape[0]
    rows = lambda width: pl.BlockSpec((block, width), lambda b: (b, 0))
    out = pl.BlockSpec((heads, block, HEAD_DIM), lambda b: (0, b, 0))
    return pl.pallas_call(
        lambda *refs: rope_kernel(heads, *refs),
        out_shape=[jax.ShapeDtypeStruct((heads, n, HEAD_DIM), BF16)] * 3,
        grid=(n // block,),
        in_specs=[rows(3 * HEAD_DIM)] * heads
        + [rows(2), pl.BlockSpec((heads, 2, HEAD_DIM), lambda b: (0, 0, 0)), rows(2 * HEAD_DIM)],
        out_specs=[out] * 3,
        compiler_params=pltpu.CompilerParams(vmem_limit_bytes=VMEM),
        cost_estimate=pl.CostEstimate(flops=heads * n * 2000, bytes_accessed=heads * n * 2304, transcendentals=0),
        name="rope",
    )(*raws, inv, gain, turn)


def rope_back_kernel(heads, *refs):
    raws, (dq_ref, dk_ref, dv_ref, inv_ref, mean_ref, gain_ref, turn_ref) = refs[:heads], refs[heads : heads + 7]
    outs, grad_ref = refs[heads + 7 : -1], refs[-1]

    @pl.when(pl.program_id(0) == 0)
    def _():
        grad_ref[...] = jnp.zeros_like(grad_ref)

    cosines, sines = turn_ref[:, :HEAD_DIM], turn_ref[:, HEAD_DIM:]
    for t in range(heads):
        for i, grad in enumerate((dq_ref, dk_ref)):
            part = slice(i * HEAD_DIM, (i + 1) * HEAD_DIM)
            inv = inv_ref[:, i : i + 1]
            hat = raws[t][:, part] * inv
            back = grad[t] * cosines - turn_half(grad[t]) * sines
            grad_ref[t, i : i + 1, :] += jnp.sum(back * hat, axis=0, keepdims=True)
            outs[t][:, part] = to_low(inv * (back * gain_ref[t, i : i + 1, :] - hat * mean_ref[:, i : i + 1]))
        outs[t][:, 2 * HEAD_DIM :] = to_low(dv_ref[t])


def rope_back(raws, dq, dk, dv, inv, mean, gain, turn, block=256):
    heads = len(raws)
    n = raws[0].shape[0]
    rows = lambda width: pl.BlockSpec((block, width), lambda b: (b, 0))
    grad = pl.BlockSpec((heads, block, HEAD_DIM), lambda b: (0, b, 0))
    gains = pl.BlockSpec((heads, 2, HEAD_DIM), lambda b: (0, 0, 0))
    out = pl.pallas_call(
        lambda *refs: rope_back_kernel(heads, *refs),
        out_shape=[jax.ShapeDtypeStruct((n, 3 * HEAD_DIM), BF16)] * heads
        + [jax.ShapeDtypeStruct((heads, 2, HEAD_DIM), F32)],
        grid=(n // block,),
        in_specs=[rows(3 * HEAD_DIM)] * heads + [grad] * 3 + [rows(2), rows(2), gains, rows(2 * HEAD_DIM)],
        out_specs=[rows(3 * HEAD_DIM)] * heads + [gains],
        compiler_params=pltpu.CompilerParams(vmem_limit_bytes=WIDE_VMEM),
        cost_estimate=pl.CostEstimate(flops=heads * n * 4000, bytes_accessed=heads * n * 3840, transcendentals=0),
        name="rope_back",
    )(*raws, dq, dk, dv, inv, mean, gain, turn)
    return out[:heads], out[heads]


def body(
    tokens,
    piece_start,
    positions,
    w_query,
    w_key,
    w_value,
    w_out,
    query_gain,
    key_gain,
    attn_gain,
    w_gate,
    w_up,
    w_down,
    mlp_gain,
    cotangent,
):
    S = lax.axis_size("shard")
    R = lax.axis_size("rep")
    s = lax.axis_index("shard")
    r = lax.axis_index("rep")
    _, span, width = tokens.shape
    heads = HEADS // S
    per = HEADS // R
    own_width = width // S
    x_own = tokens.reshape(span, width)

    by_ring = per * 2 == S
    chip, core = r // 2, r % 2

    def head_columns(j):
        start = j * HEAD_DIM
        return jnp.concatenate(
            [to_low(lax.dynamic_slice_in_dim(w, start, HEAD_DIM, 1)) for w in (w_query, w_key, w_value)], axis=1
        )

    def by_core(value):
        if not by_ring:
            return value
        middle = value.shape[1] // 2
        return jnp.where(core == 1, jnp.concatenate([value[:, middle:], value[:, :middle]], axis=1), value)

    own_columns = [head_columns((s + k) % per) for k in range(per)]
    got = [permute(value, heads_perm(S, R, per, k)) for k, value in enumerate(own_columns)]
    gains_own = jnp.stack([to_low(g).astype(F32) for g in (query_gain, key_gain, attn_gain, mlp_gain)])
    small = jnp.concatenate([positions.reshape(span).astype(F32), gains_own.reshape(-1)])
    small_all = [small] + [send_shard(small, k) for k in range(1, S)]
    own_out = spread_heads(after(to_low(w_out), *own_columns).reshape(heads, HEAD_DIM, -1), s)
    got, small_all, own_out = lax.optimization_barrier((got, small_all, own_out))

    got = reverse_pick(jnp.stack(got), s % per).reshape(per * own_width, 3 * HEAD_DIM)
    if by_ring:
        qkv_pairs = gather_pairs(got, R)
        qkv_w = [jnp.concatenate(pair) for pair in qkv_pairs]
        head_order = (chip - jnp.arange(heads)) % heads
        ring_start, ring_late, ring_end = qkv_pairs[1][0], qkv_pairs[-2][0], qkv_pairs[-1][0]
    else:
        qkv_w = list(lax.all_gather(got, "rep", axis=0, tiled=True).reshape(heads, width, 3 * HEAD_DIM))
        head_order = jnp.arange(heads)
        ring_start = ring_late = ring_end = qkv_w[-1]
    where = jnp.concatenate([head_order, piece_start]).astype(jnp.int32)
    x_all, x_first = gather_tokens(by_core(after(x_own, got)), (ring_start,), (ring_late,))
    gate_up = after(jnp.concatenate([to_low(w_gate), to_low(w_up)], axis=1), x_all)
    gate_up_w = lax.all_gather(gate_up, "shard", axis=0, tiled=True)
    pieces = spread_down(after(to_low(w_down), x_first), s)

    own_out = own_out.reshape(own_width, -1)
    columns = own_out.shape[1]
    out_w = jnp.zeros((own_width, width), BF16)
    for t, pair in enumerate(gather_pairs(after(own_out, ring_end), R)):
        for i, block in enumerate(pair):
            start = ((chip - t) % (R // 2) * 2 + (core ^ i)) * columns
            out_w = lax.dynamic_update_slice_in_dim(out_w, block, start, 1)
    down_blocks = cross_down([after(piece, out_w) for piece in pieces], s, r)

    gains = unrelative(jnp.stack([v[span:].reshape(4, own_width) for v in small_all]), s)
    gains = gains.transpose(1, 0, 2).reshape(4, width)
    head_gains = gains[:2].reshape(2, heads, S, HEAD_DIM)
    head_gains = lax.dynamic_index_in_dim(head_gains, s, 2, keepdims=False)
    head_gains = head_gains.transpose(1, 0, 2)
    if by_ring:
        head_gains = reverse_pick(head_gains, chip)
    again, mgain = gains[2], gains[3]
    order = token_order(S)
    step = S * span // len(order)
    place_pos = jnp.concatenate([small_all[j][h * step : (h + 1) * step] for h, j in order])
    place = jnp.concatenate([(s ^ j) * span + h * step + lax.iota(jnp.int32, step) for h, j in order])
    angles = place_pos[:, None] * frequencies()
    cosines, sines = jnp.cos(angles), jnp.sin(angles)
    turn = jnp.concatenate([cosines, cosines, -sines, sines], axis=1)

    raws = [mm(x_all, w) for w in qkv_w]
    inv = lax.rsqrt(sum_rows(squares(raws)) / width + epsilon).T
    q, k, v = rope(raws, inv, head_gains, turn)
    o = attend(q, k, v, place, where)
    rows = S * span // 2
    a_send = mm(o[rows:], out_w)
    a_keep = mm(o[:rows], out_w)
    down_blocks = [after(b, o) for b in down_blocks]
    a = scatter_tokens(a_keep, a_send, down_blocks)
    ainv = lax.rsqrt(jnp.mean(a * a, axis=-1, keepdims=True) + epsilon)
    ahat = a * ainv
    h = x_own.astype(F32) + ahat * again
    hb = to_low(h)

    down_w = lax.all_gather(join_down([after(b, hb) for b in down_blocks], r), "shard", axis=0, tiled=True)
    hb_pairs = [jnp.concatenate(pair) for pair in gather_pairs(hb, R)]
    kept = {}
    ff = w_gate.shape[1]

    def forward(t, hold):
        if t not in kept:
            pair = hb_pairs[t] if hold is None else after(hb_pairs[t], hold)
            gu = mm(pair, gate_up_w)
            g, u = gu[:, :ff], gu[:, ff:]
            inner = to_low(g * jax.nn.sigmoid(g) * u)
            kept[t] = (g, u, inner, mm(inner, down_w))
        return kept[t][3]

    forward(0, None)
    z = scatter_pairs(forward, R)
    zinv = lax.rsqrt(jnp.mean(z * z, axis=-1, keepdims=True) + epsilon)
    zhat = z * zinv
    output = to_low(h + zhat * mgain).reshape(tokens.shape)

    dy = cotangent.reshape(span, width).astype(F32)
    grad_mgain = jnp.sum(dy * zhat, axis=0)
    scaled = dy * mgain
    dz = to_low(zinv * (scaled - zhat * jnp.mean(scaled * zhat, axis=-1, keepdims=True)))
    dz_pairs = [jnp.concatenate(pair) for pair in gather_pairs(dz, R)]
    grads = {}

    def backward(t, hold):
        if t not in grads:
            pair = dz_pairs[t] if hold is None else after(dz_pairs[t], hold)
            g, u = kept[t][:2]
            dm = mm_last(pair, down_w)
            sig = jax.nn.sigmoid(g)
            dg = to_low(dm * u * sig * (1.0 + g * (1.0 - sig)))
            du = to_low(dm * g * sig)
            dgu = jnp.concatenate([dg, du], axis=1)
            grads[t] = (dgu, mm_last(dgu, gate_up_w))
        return grads[t][1]

    weight_grads = {}

    def weight_grad(i, _):
        steps = range(len(kept))
        if i == 0:
            all_inner = jnp.concatenate([kept[t][2] for t in steps])
            down_grad = to_low(mm_first(all_inner, jnp.concatenate(dz_pairs)))
            share = lax.psum_scatter(down_grad, "shard", scatter_dimension=0, tiled=True)
            weight_grads.update(down=down_grad, down_share=share)
            return (down_grad,)
        if i == len(kept) - 2:
            hb_all = jnp.concatenate(hb_pairs)
            weight_grads["gate_up"] = to_low(mm_first(hb_all, jnp.concatenate([grads[t][0] for t in steps])))
            return (weight_grads["gate_up"], weight_grads["down_share"])
        return ()

    backward(0, None)
    dh = dy + scatter_pairs(backward, R, weight_grad)
    grad_again = jnp.sum(dh * ahat, axis=0)
    scaled = dh * again
    da = to_low(ainv * (scaled - ahat * jnp.mean(scaled * ahat, axis=-1, keepdims=True)))
    down_back = return_cross(weight_grads["down_share"], r)
    da_all, _ = gather_tokens(da, down_back[: R // 2], down_back[R // 2 :])
    do = to_low(mm_last(da_all, out_w))
    gate_up_grad = after(weight_grads["gate_up"], da_all)
    gate_up_share = lax.psum_scatter(gate_up_grad, "shard", scatter_dimension=0, tiled=True).astype(F32)
    dq, dk, dv = attend_back(q, k, v, do, place, where)
    means = (sum_rows(inner_products(dq, q, dk, k)) / width).T
    dqkv, head_grads = rope_back(raws, dq, dk, dv, inv, means, head_gains, turn)
    if by_ring:
        head_grads = reverse_pick(head_grads, chip)
    down_back = return_spread(down_back, s, r)
    wide = jnp.stack([grad_again, grad_mgain]).reshape(2, S, own_width).transpose(1, 0, 2)
    wide = jnp.sum(exchange_shard(after(wide, dqkv[0]), s), axis=0)
    gain_sums = sum_rep(jnp.concatenate([head_grads.reshape(2, -1), wide], axis=1))
    out_grad = to_low(mm_first(o, after(da_all, *dqkv)))
    out_grad = after(out_grad, gate_up_share)

    late = {}

    def qkv_part(t, hold):
        return mm_first(x_all, dqkv[t] if hold is None else after(dqkv[t], hold))

    def input_grad(i, hold=None):
        if i < 2:
            part = slice(rows, None) if i == 0 else slice(rows)
            held = [d if hold is None else after(d, hold) for d in dqkv]
            late[i] = sum(mm_last(d[part], w) for d, w in zip(held, qkv_w))
            return (late[i], gain_sums) if i else (late[i], *down_back)
        return ()

    if by_ring:
        qkv_share = to_low(scatter_pairs(qkv_part, R, input_grad))
    else:
        parts = jnp.concatenate([qkv_part(t, None) for t in range(heads)])
        qkv_share = lax.psum_scatter(to_low(parts), "rep", scatter_dimension=0, tiled=True)
        input_grad(0), input_grad(1)
    dx = dh + by_core(scatter_tokens(late[1], late[0], (), (qkv_share,)))

    out_share = lax.psum_scatter(out_grad, "rep", scatter_dimension=1, tiled=True)
    grad_out = collect_heads(out_share.reshape(heads, HEAD_DIM, -1), s).reshape(w_out.shape).astype(F32)
    slots = qkv_share.reshape(per, own_width, 3 * HEAD_DIM)
    back = jnp.stack([permute(pick(slots, (s - k) % per), flip(heads_perm(S, R, per, k))) for k in range(per)])
    back = roll_pick(back, -(s % per)).reshape(per, own_width, 3, HEAD_DIM)
    back = back.transpose(2, 1, 0, 3).reshape(3, own_width, per * HEAD_DIM).astype(F32)

    grad_down = place_units(down_back, s).astype(F32)
    gain_sums = after(gain_sums, qkv_share)
    head_grads = collect_heads(gain_sums[:, : heads * HEAD_DIM].reshape(heads, 2, HEAD_DIM), s)
    head_grads = head_grads.transpose(1, 0, 2).reshape(2, own_width)
    gain_grads = jnp.concatenate([head_grads, gain_sums[:, heads * HEAD_DIM :]])

    return (
        output,
        dx.reshape(tokens.shape),
        back[0],
        back[1],
        back[2],
        grad_out,
        gain_grads[0],
        gain_grads[1],
        gain_grads[2],
        gate_up_share[:, :ff],
        gate_up_share[:, ff:],
        grad_down,
        gain_grads[3],
    )


def solution(mesh):
    grid = P("shard", "rep")
    rows = P("rep", "shard", None)
    gain = P("shard")
    in_specs = (rows, P("rep"), P("rep", "shard"), grid, grid, grid, grid, gain, gain, gain, grid, grid, grid, gain, rows)
    out_specs = (rows, rows, grid, grid, grid, grid, gain, gain, gain, grid, grid, grid, gain)
    return jax.shard_map(body, mesh=mesh, in_specs=in_specs, out_specs=out_specs, check_vma=False)
```

```python
import jax
import jax.numpy as jnp
from jax import lax
from jax.experimental import pallas as pl
from jax.experimental.pallas import tpu as pltpu
from jax.sharding import PartitionSpec as P

HEADS = 16
HEAD_DIM = 128
PIECE = 256
SCALE = HEAD_DIM ** (-0.5)

LOG2_E = 1.4426950408889634
VMEM = 24 << 20
WIDE_VMEM = 56 << 20

epsilon = 1e-06
rope_base = 500000.0

F32 = jnp.float32
BF16 = jnp.bfloat16

SQUARE = ((0, 0), (0, 2), (1, 0), (1, 1), (0, 1), (0, 3), (1, 2), (1, 3))


def token_order(count):
    return SQUARE if count == 4 else tuple((0, j) for j in range(count))


def to_low(tensor):
    return tensor.astype(BF16)


def dot(left, right, contract):
    return lax.dot_general(left, right, ((contract[0], contract[1]), ((), ())), preferred_element_type=F32)


def mm(left, right):
    return dot(left, right, ((1,), (0,)))


def mm_first(left, right):
    return dot(left, right, ((0,), (0,)))


def mm_last(left, right):
    return dot(left, right, ((1,), (1,)))


def after(value, *others):
    return lax.optimization_barrier((value,) + others)[0]


def send_shard(value, k):
    count = lax.axis_size("shard")
    return lax.ppermute(value, "shard", [(s, s ^ k) for s in range(count)])


def gather_tokens(own, first_hold=(), last_hold=()):
    count = lax.axis_size("shard")
    if count != 4:
        others = [send_shard(own, k) for k in range(1, count)]
        return jnp.concatenate([own] + others), others[0]
    half = own.shape[0] // 2
    a0, b0 = own[:half], own[half:]
    a2 = send_shard(a0, 2)
    b1 = send_shard(b0, 1)
    if first_hold:
        a2, b1 = after(a2, *first_hold), after(b1, *first_hold)
    a02 = jnp.concatenate([a0, a2])
    b01 = jnp.concatenate([b0, b1])
    a13 = send_shard(a02, 1)
    b23 = send_shard(b01, 2)
    last = a13
    if last_hold:
        a13, b23 = after(a13, *last_hold), after(b23, *last_hold)
    return jnp.concatenate([a02, b01, a13, b23]), last


def scatter_tokens(keep, send, first_hold=(), last_hold=()):
    count = lax.axis_size("shard")
    if count != 4:
        parts = jnp.split(jnp.concatenate([keep, send]), count)
        return parts[0] + sum(send_shard(to_low(parts[k]), k).astype(F32) for k in range(1, count))
    q = keep.shape[0] // 2
    send_low = to_low(send)
    a_in = send_shard(send_low[:q], 1)
    b_in = send_shard(send_low[q:], 2)
    if first_hold:
        a_in, b_in = after(a_in, *first_hold), after(b_in, *first_hold)
    a02 = keep[:q] + a_in.astype(F32)
    b01 = keep[q:] + b_in.astype(F32)
    h = q // 2
    a_last = send_shard(to_low(a02[h:]), 2)
    b_last = send_shard(to_low(b01[h:]), 1)
    if last_hold:
        a_last, b_last = after(a_last, *last_hold), after(b_last, *last_hold)
    return jnp.concatenate([a02[:h] + a_last.astype(F32), b01[:h] + b_last.astype(F32)])


def swap_blocks(rows, k):
    order = token_order(lax.axis_size("shard"))
    step = rows.shape[-1] // len(order)
    index = [order.index((h, j ^ k)) for h, j in order]
    return jnp.concatenate([rows[..., i * step : (i + 1) * step] for i in index], axis=-1)


def sum_rows(rows):
    return rows + sum(swap_blocks(send_shard(rows, k), k) for k in range(1, lax.axis_size("shard")))


def unrelative(blocks, s):
    shape = blocks.shape
    bits = shape[0].bit_length() - 1
    cube = blocks.reshape((2,) * bits + shape[1:])
    for bit in range(bits):
        cube = jnp.where((s >> bit) % 2 == 1, jnp.flip(cube, bits - 1 - bit), cube)
    return cube.reshape(shape)


def exchange(blocks, axis):
    return lax.all_to_all(blocks, axis, 0, 0, tiled=True)


def rows_perm(count, heads, k):
    c = count // heads
    return [(s, heads * (s % c) + (s // c + k) % heads) for s in range(count)]


def spread_heads(blocks, s):
    heads, count = blocks.shape[0], lax.axis_size("shard")
    if heads == count:
        return exchange(blocks, "shard")
    q = s // (count // heads)
    got = [lax.ppermute(pick(blocks, (q + k) % heads), "shard", rows_perm(count, heads, k)) for k in range(heads)]
    return reverse_pick(jnp.stack(got), s % heads)


def collect_heads(blocks, s):
    heads, count = blocks.shape[0], lax.axis_size("shard")
    if heads == count:
        return exchange(blocks, "shard")
    q = s // (count // heads)
    got = [
        lax.ppermute(pick(blocks, (s - k) % heads), "shard", flip(rows_perm(count, heads, k))) for k in range(heads)
    ]
    return roll_pick(jnp.stack(got), -q)


def ring(value, count):
    return lax.ppermute(value, "rep", [(r, (r + 2) % count) for r in range(count)])


def sibling(value, count):
    return lax.ppermute(value, "rep", [(r, r ^ 1) for r in range(count)])


def gather_pairs(own, count):
    blocks = [own]
    for _ in range(count // 2 - 1):
        blocks.append(ring(blocks[-1], count))
    pairs = []
    for i, block in enumerate(blocks):
        other = sibling(block, count)
        pairs.append((block, after(other, blocks[i + 1]) if i + 1 < len(blocks) else other))
    return pairs


def scatter_pairs(part_of, count, beside=lambda i, low: ()):
    total = low = None
    for i, step in enumerate(list(range(1, count // 2)) + [0]):
        part = part_of(step, low)
        half = part.shape[0] // 2
        mine = part[:half].astype(F32) + sibling(to_low(part[half:]), count).astype(F32)
        if total is None:
            total = mine
        else:
            got = ring(low, count)
            hold = beside(i - 1, low)
            if hold:
                got = after(got, *hold)
            total = got.astype(F32) + mine
        low = to_low(total)
    return total


def round_the_ring(own, compute, count, early, late):
    chips = count // 2

    def mine(part):
        middle = part.shape[0] // 2
        return part[:middle] + sibling(to_low(part[middle:]), count).astype(F32)

    block, parts, total = own, [], None
    for t in range(chips):
        following = ring(block, count) if t + 1 < chips else None
        parts.append(compute(t, jnp.concatenate([block, sibling(block, count)])))
        if t == 1:
            total = mine(parts[1])
        if following is not None:
            hold = early(t) + ((to_low(total),) if t == chips - 2 else ())
            block = after(following, *hold) if hold else following
    for step, t in enumerate(list(range(2, chips)) + [0]):
        low = to_low(total)
        got = ring(low, count)
        hold = late(step, low)
        if hold:
            got = after(got, *hold)
        total = got.astype(F32) + mine(parts[t])
    return total


def heads_perm(shard_count, rep_count, per, k):
    group = shard_count // per
    pairs = []
    for r in range(rep_count):
        for s in range(shard_count):
            j = (s % per + k) % per
            target = (r // group * group + s // per, per * (r % group) + j)
            pairs.append((r * shard_count + s, target[0] * shard_count + target[1]))
    return pairs


def flip_rep(value, d):
    count = lax.axis_size("rep")
    return lax.ppermute(value, "rep", [(i, i ^ d) for i in range(count)])


def sum_rep(value):
    d = 1
    while d < lax.axis_size("rep"):
        value = value + flip_rep(value, d)
        d *= 2
    return value


def spread_down(rows):
    S, R = lax.axis_size("shard"), lax.axis_size("rep")
    share, columns = rows.shape[0] // R, rows.shape[1]
    units = rows.reshape(R // S, S, share, columns).transpose(1, 0, 2, 3)
    return exchange(units, "shard").reshape(R, share, columns)


def join_down(pieces):
    R, share, columns = pieces.shape
    return pieces.transpose(1, 0, 2).reshape(share, R * columns)


def part_down(rows):
    share, R = rows.shape[0], lax.axis_size("rep")
    return rows.reshape(share, R, -1).transpose(1, 0, 2)


def collect_down(pieces):
    R, share, columns = pieces.shape
    S = lax.axis_size("shard")
    units = exchange(pieces.reshape(S, R // S, share, columns), "shard")
    return units.transpose(1, 0, 2, 3).reshape(R * share, columns)


def flip(pairs):
    return [(b, a) for a, b in pairs]


def permute(value, pairs):
    return lax.ppermute(value, ("rep", "shard"), pairs)


def pick(values, index):
    return lax.dynamic_index_in_dim(values, index, 0, keepdims=False)


def roll_pick(values, shift):
    n = values.shape[0]
    if n == 1:
        return values
    return lax.dynamic_slice_in_dim(jnp.concatenate([values, values]), shift % n, n, 0)


def reverse_pick(values, base):
    n = values.shape[0]
    if n == 1:
        return values
    return roll_pick(values[::-1], n - 1 - base)


def frequencies():
    return jnp.power(jnp.float32(rope_base), -2.0 * jnp.arange(HEAD_DIM // 2, dtype=F32) / HEAD_DIM)


def bias_of(piece_first, row, col):
    row_in = (row >= piece_first) & (row < piece_first + PIECE)
    col_in = (col >= piece_first) & (col < piece_first + PIECE)
    return jnp.where((col <= row) | (row_in & col_in), 0.0, -1e30).astype(F32)


def attend_kernel(where_ref, q_ref, k_ref, v_ref, row_ref, col_ref, o_ref, bias_ref):
    @pl.when(pl.program_id(1) == 0)
    def _():
        bias_ref[...] = bias_of(where_ref[where_ref.shape[0] - 1], row_ref[...], col_ref[...])

    scores = mm_last(q_ref[0], k_ref[0]) * (SCALE * LOG2_E) + bias_ref[...]
    powers = jnp.exp2(scores - jnp.max(scores, axis=-1, keepdims=True))
    weights = powers * (1.0 / jnp.sum(powers, axis=-1, keepdims=True))
    o_ref[...] = to_low(mm(to_low(weights), v_ref[0]))


def attend(q, k, v, place, where, block=256):
    heads, n, hd = q.shape
    whole = pl.BlockSpec((1, n, hd), lambda b, t, w: (t, 0, 0))
    return pl.pallas_call(
        attend_kernel,
        out_shape=jax.ShapeDtypeStruct((n, heads * hd), BF16),
        grid_spec=pltpu.PrefetchScalarGridSpec(
            num_scalar_prefetch=1,
            grid=(n // block, heads),
            in_specs=[
                pl.BlockSpec((1, block, hd), lambda b, t, w: (t, b, 0)),
                whole,
                whole,
                pl.BlockSpec((block, 1), lambda b, t, w: (b, 0)),
                pl.BlockSpec((1, n), lambda b, t, w: (0, 0)),
            ],
            out_specs=pl.BlockSpec((block, hd), lambda b, t, w: (b, w[t])),
            scratch_shapes=[pltpu.VMEM((block, n), F32)],
        ),
        compiler_params=pltpu.CompilerParams(vmem_limit_bytes=VMEM),
        cost_estimate=pl.CostEstimate(
            flops=4 * heads * n * n * hd, bytes_accessed=8 * heads * n * hd, transcendentals=heads * n * n
        ),
        name="attend",
    )(where, q, k, v, place[:, None], place[None, :])


def attend_back_kernel(where_ref, q_ref, k_ref, v_ref, do_ref, row_ref, col_ref, dq_ref, dk_ref, dv_ref, products_ref, bias_ref):
    t, b = pl.program_id(0), pl.program_id(1)

    @pl.when(pl.program_id(0) == 0)
    def _():
        bias_ref[b] = bias_of(where_ref[where_ref.shape[0] - 1], row_ref[...], col_ref[...])

    q, k, v, do = q_ref[0], k_ref[0], v_ref[0], do_ref[...]
    scores = mm_last(k, q) * (SCALE * LOG2_E) + bias_ref[b]
    powers = jnp.exp2(scores - jnp.max(scores, axis=0, keepdims=True))
    probs = powers * (1.0 / jnp.sum(powers, axis=0, keepdims=True))
    grad_probs = mm_last(v, do)
    delta = jnp.sum(probs * grad_probs, axis=0, keepdims=True)
    grad_scores = to_low(probs * (grad_probs - delta))
    dq = mm_first(grad_scores, k) * SCALE
    dq_ref[0] = dq
    dk = mm(grad_scores, q) * SCALE
    dv = mm(to_low(probs), do)

    @pl.when((t == 0) & (b == 0))
    def _():
        products_ref[...] = jnp.zeros_like(products_ref)

    own = pl.ds(pl.multiple_of(b * q.shape[0], q.shape[0]), q.shape[0])
    products_ref[0:1, own] += jnp.sum((dq * q.astype(F32)).T, axis=0, keepdims=True)

    @pl.when(b == 0)
    def _():
        dk_ref[0] = dk
        dv_ref[0] = dv

    @pl.when(b > 0)
    def _():
        dk_ref[0] += dk
        dv_ref[0] += dv

    @pl.when(b == pl.num_programs(1) - 1)
    def _():
        products_ref[1:2, :] += jnp.sum((dk_ref[0] * k.astype(F32)).T, axis=0, keepdims=True)


def attend_back(q, k, v, do, place, where, block=512):
    heads, n, hd = q.shape
    one = pl.BlockSpec((1, block, hd), lambda t, b, w: (t, b, 0))
    whole = pl.BlockSpec((1, n, hd), lambda t, b, w: (t, 0, 0))
    return pl.pallas_call(
        attend_back_kernel,
        out_shape=[jax.ShapeDtypeStruct((heads, n, hd), F32)] * 3 + [jax.ShapeDtypeStruct((2, n), F32)],
        grid_spec=pltpu.PrefetchScalarGridSpec(
            num_scalar_prefetch=1,
            grid=(heads, n // block),
            in_specs=[
                one,
                whole,
                whole,
                pl.BlockSpec((block, hd), lambda t, b, w: (b, w[t])),
                pl.BlockSpec((1, block), lambda t, b, w: (0, b)),
                pl.BlockSpec((n, 1), lambda t, b, w: (0, 0)),
            ],
            out_specs=[one, whole, whole, pl.BlockSpec((2, n), lambda t, b, w: (0, 0))],
            scratch_shapes=[pltpu.VMEM((n // block, n, block), F32)],
        ),
        compiler_params=pltpu.CompilerParams(vmem_limit_bytes=32 << 20),
        cost_estimate=pl.CostEstimate(
            flops=10 * heads * n * n * hd, bytes_accessed=20 * heads * n * hd, transcendentals=heads * n * n
        ),
        name="attend_back",
    )(where, q, k, v, do, place[None, :], place[:, None])


def columns_of(t, i):
    return slice((3 * t + i) * HEAD_DIM, (3 * t + i + 1) * HEAD_DIM)


def squares_kernel(heads, raw_ref, out_ref):
    for i in (0, 1):
        total = sum(jnp.square(raw_ref[:, columns_of(t, i)]) for t in range(heads))
        out_ref[i : i + 1, :] = jnp.sum(total.T, axis=0, keepdims=True)


def squares(raw, heads, block=256):
    n, width = raw.shape
    return pl.pallas_call(
        lambda *refs: squares_kernel(heads, *refs),
        out_shape=jax.ShapeDtypeStruct((2, n), F32),
        grid=(n // block,),
        in_specs=[pl.BlockSpec((block, width), lambda b: (b, 0))],
        out_specs=pl.BlockSpec((2, block), lambda b: (0, b)),
        compiler_params=pltpu.CompilerParams(vmem_limit_bytes=VMEM),
        cost_estimate=pl.CostEstimate(flops=heads * n * 512, bytes_accessed=heads * n * 1536, transcendentals=0),
        name="squares",
    )(raw)


def turn_half(tensor):
    return pltpu.roll(tensor, HEAD_DIM // 2, 1)


def rope_kernel(heads, raw_ref, inv_ref, gain_ref, turn_ref, q_ref, k_ref, v_ref):
    cosines, sines = turn_ref[:, :HEAD_DIM], turn_ref[:, HEAD_DIM:]
    for t in range(heads):
        for i, out in enumerate((q_ref, k_ref)):
            value = raw_ref[:, columns_of(t, i)] * inv_ref[:, i : i + 1] * gain_ref[t, i : i + 1, :]
            out[t] = to_low(value * cosines + turn_half(value) * sines)
        v_ref[t] = to_low(raw_ref[:, columns_of(t, 2)])


def rope(raw, inv, gain, turn, block=256):
    heads, n = gain.shape[0], raw.shape[0]
    rows = lambda width: pl.BlockSpec((block, width), lambda b: (b, 0))
    out = pl.BlockSpec((heads, block, HEAD_DIM), lambda b: (0, b, 0))
    return pl.pallas_call(
        lambda *refs: rope_kernel(heads, *refs),
        out_shape=[jax.ShapeDtypeStruct((heads, n, HEAD_DIM), BF16)] * 3,
        grid=(n // block,),
        in_specs=[
            rows(raw.shape[1]),
            rows(2),
            pl.BlockSpec((heads, 2, HEAD_DIM), lambda b: (0, 0, 0)),
            rows(2 * HEAD_DIM),
        ],
        out_specs=[out] * 3,
        compiler_params=pltpu.CompilerParams(vmem_limit_bytes=VMEM),
        cost_estimate=pl.CostEstimate(flops=heads * n * 2000, bytes_accessed=heads * n * 2304, transcendentals=0),
        name="rope",
    )(raw, inv, gain, turn)


def rope_back_kernel(
    heads, raw_ref, dq_ref, dk_ref, dv_ref, inv_ref, mean_ref, gain_ref, turn_ref, out_ref, grad_ref
):
    @pl.when(pl.program_id(0) == 0)
    def _():
        grad_ref[...] = jnp.zeros_like(grad_ref)

    cosines, sines = turn_ref[:, :HEAD_DIM], turn_ref[:, HEAD_DIM:]
    for t in range(heads):
        for i, grad in enumerate((dq_ref, dk_ref)):
            inv = inv_ref[:, i : i + 1]
            hat = raw_ref[:, columns_of(t, i)] * inv
            back = grad[t] * cosines - turn_half(grad[t]) * sines
            grad_ref[t, i : i + 1, :] += jnp.sum(back * hat, axis=0, keepdims=True)
            row = inv * (back * gain_ref[t, i : i + 1, :] - hat * mean_ref[:, i : i + 1])
            out_ref[:, columns_of(t, i)] = to_low(row)
        out_ref[:, columns_of(t, 2)] = to_low(dv_ref[t])


def rope_back(raw, dq, dk, dv, inv, mean, gain, turn, block=256):
    heads, (n, width) = gain.shape[0], raw.shape
    rows = lambda width: pl.BlockSpec((block, width), lambda b: (b, 0))
    grad = pl.BlockSpec((heads, block, HEAD_DIM), lambda b: (0, b, 0))
    gains = pl.BlockSpec((heads, 2, HEAD_DIM), lambda b: (0, 0, 0))
    return pl.pallas_call(
        lambda *refs: rope_back_kernel(heads, *refs),
        out_shape=[jax.ShapeDtypeStruct((n, width), BF16), jax.ShapeDtypeStruct((heads, 2, HEAD_DIM), F32)],
        grid=(n // block,),
        in_specs=[rows(width)] + [grad] * 3 + [rows(2), rows(2), gains, rows(2 * HEAD_DIM)],
        out_specs=[rows(width), gains],
        compiler_params=pltpu.CompilerParams(vmem_limit_bytes=WIDE_VMEM),
        cost_estimate=pl.CostEstimate(flops=heads * n * 4000, bytes_accessed=heads * n * 3840, transcendentals=0),
        name="rope_back",
    )(raw, dq, dk, dv, inv, mean, gain, turn)


def body(
    tokens,
    piece_start,
    positions,
    w_query,
    w_key,
    w_value,
    w_out,
    query_gain,
    key_gain,
    attn_gain,
    w_gate,
    w_up,
    w_down,
    mlp_gain,
    cotangent,
):
    S = lax.axis_size("shard")
    R = lax.axis_size("rep")
    s = lax.axis_index("shard")
    r = lax.axis_index("rep")
    _, span, width = tokens.shape
    heads = HEADS // S
    per = HEADS // R
    own_width = width // S
    x_own = tokens.reshape(span, width)

    by_ring = per * 2 == S
    chip, core = r // 2, r % 2

    def head_columns(j):
        start = j * HEAD_DIM
        return jnp.concatenate(
            [to_low(lax.dynamic_slice_in_dim(w, start, HEAD_DIM, 1)) for w in (w_query, w_key, w_value)], axis=1
        )

    def by_core(value):
        if not by_ring:
            return value
        middle = value.shape[1] // 2
        return jnp.where(core == 1, jnp.concatenate([value[:, middle:], value[:, :middle]], axis=1), value)

    own_columns = [head_columns((s + k) % per) for k in range(per)]
    got = [permute(value, heads_perm(S, R, per, k)) for k, value in enumerate(own_columns)]
    gains_own = jnp.stack([to_low(g).astype(F32) for g in (query_gain, key_gain, attn_gain, mlp_gain)])
    small = jnp.concatenate([positions.reshape(span).astype(F32), gains_own.reshape(-1)])
    small_all = [small] + [send_shard(small, k) for k in range(1, S)]
    own_out = spread_heads(after(to_low(w_out), *own_columns).reshape(heads, HEAD_DIM, -1), s)
    got, small_all, own_out = lax.optimization_barrier((got, small_all, own_out))

    got = reverse_pick(jnp.stack(got), s % per).reshape(per * own_width, 3 * HEAD_DIM)
    if by_ring:
        qkv_pairs = gather_pairs(got, R)
        qkv_w = jnp.zeros((width, heads * 3 * HEAD_DIM), BF16)
        for t, pair in enumerate(qkv_pairs):
            for i, block in enumerate(pair):
                qkv_w = lax.dynamic_update_slice(qkv_w, block, (i * block.shape[0], t * block.shape[1]))
        head_order = (chip - jnp.arange(heads)) % heads
        ring_start, ring_late, ring_end = qkv_pairs[1][0], qkv_pairs[-2][0], qkv_pairs[-1][0]
    else:
        qkv_w = lax.all_gather(got, "rep", axis=0, tiled=True).reshape(heads, width, 3 * HEAD_DIM)
        qkv_w = jnp.concatenate(list(qkv_w), axis=1)
        head_order = jnp.arange(heads)
        ring_start = ring_late = ring_end = qkv_w
    where = jnp.concatenate([head_order, piece_start]).astype(jnp.int32)
    x_all, x_last = gather_tokens(by_core(after(x_own, got)), (ring_start,), (ring_late,))
    gate_up = after(jnp.concatenate([to_low(w_gate), to_low(w_up)], axis=1), x_last)
    gate_up_w = lax.all_gather(gate_up, "shard", axis=0, tiled=True)

    own_out = own_out.reshape(own_width, -1)
    columns = own_out.shape[1]

    gains = unrelative(jnp.stack([v[span:].reshape(4, own_width) for v in small_all]), s)
    gains = gains.transpose(1, 0, 2).reshape(4, width)
    head_gains = gains[:2].reshape(2, heads, S, HEAD_DIM)
    head_gains = lax.dynamic_index_in_dim(head_gains, s, 2, keepdims=False)
    head_gains = head_gains.transpose(1, 0, 2)
    if by_ring:
        head_gains = reverse_pick(head_gains, chip)
    again, mgain = gains[2], gains[3]
    order = token_order(S)
    step = S * span // len(order)
    place_pos = jnp.concatenate([small_all[j][h * step : (h + 1) * step] for h, j in order])
    place = jnp.concatenate([(s ^ j) * span + h * step + lax.iota(jnp.int32, step) for h, j in order])
    angles = place_pos[:, None] * frequencies()
    cosines, sines = jnp.cos(angles), jnp.sin(angles)
    turn = jnp.concatenate([cosines, cosines, -sines, sines], axis=1)

    raw = mm(x_all, qkv_w)
    pieces = spread_down(after(to_low(w_down), raw))
    raw_squares = squares(raw, heads)
    inv = lax.rsqrt(sum_rows(raw_squares) / width + epsilon).T
    q, k, v = rope(raw, inv, head_gains, turn)
    o = attend(q, k, v, place, where)

    out_w = jnp.zeros((own_width, width), BF16)
    block = after(own_out, ring_end)
    for t in range(R // 2):
        if t:
            block = after(ring(block, R), (raw_squares, q, o)[min(t - 1, 2)])
        for i, value in enumerate((block, sibling(block, R))):
            start = ((chip - t) % (R // 2) * 2 + (core ^ i)) * columns
            out_w = lax.dynamic_update_slice_in_dim(out_w, value, start, 1)
    rows = S * span // 2
    a_send = mm(o[rows:], out_w)
    a_keep = mm(o[:rows], out_w)
    down_blocks = exchange(after(pieces, a_send), "rep")
    a = scatter_tokens(a_keep, a_send, (down_blocks,))
    ainv = lax.rsqrt(jnp.mean(a * a, axis=-1, keepdims=True) + epsilon)
    ahat = a * ainv
    h = x_own.astype(F32) + ahat * again
    hb = to_low(h)

    down_w = lax.all_gather(join_down(after(down_blocks, hb)), "shard", axis=0, tiled=True)
    chips, ff = R // 2, w_gate.shape[1]
    kept = {}

    def forward(t, pair):
        gu = mm(pair, gate_up_w)
        g, u = gu[:, :ff], gu[:, ff:]
        inner = to_low(g * jax.nn.sigmoid(g) * u)
        kept[t] = (g, u, inner, pair)
        return mm(inner, down_w)

    z = round_the_ring(hb, forward, R, lambda t: (), lambda step, low: ())
    zinv = lax.rsqrt(jnp.mean(z * z, axis=-1, keepdims=True) + epsilon)
    zhat = z * zinv
    output = to_low(h + zhat * mgain).reshape(tokens.shape)

    dy = cotangent.reshape(span, width).astype(F32)
    grad_mgain = jnp.sum(dy * zhat, axis=0)
    scaled = dy * mgain
    dz = to_low(zinv * (scaled - zhat * jnp.mean(scaled * zhat, axis=-1, keepdims=True)))
    dgs, dus, dz_pairs, dh_parts, weight_grads = {}, {}, {}, {}, {}

    def backward(t, pair):
        g, u = kept[t][:2]
        dm = mm_last(pair, down_w)
        sig = jax.nn.sigmoid(g)
        dz_pairs[t] = pair
        dgs[t] = to_low(dm * u * sig * (1.0 + g * (1.0 - sig)))
        dus[t] = to_low(dm * g * sig)
        dh_parts[t] = mm_last(jnp.concatenate([dgs[t], dus[t]], axis=1), gate_up_w)
        return dh_parts[t]

    def all_tokens(values):
        return jnp.concatenate([values[t] for t in range(chips)])

    def weight_grad(step, low):
        hold = (dh_parts[chips - 1],) if step == 0 else ()
        if step == chips - 3:
            inner_all = after(jnp.concatenate([kept[t][2] for t in range(chips)]), low)
            down_grad = to_low(mm_first(inner_all, all_tokens(dz_pairs)))
            weight_grads["down"] = down_grad
            weight_grads["down_share"] = lax.psum_scatter(down_grad, "shard", scatter_dimension=0, tiled=True)
            hold += (down_grad,)
        if step == chips - 2:
            hb_all = after(jnp.concatenate([kept[t][3] for t in range(chips)]), low)
            weight_grads["gate"] = to_low(mm_first(hb_all, all_tokens(dgs)))
            weight_grads["up"] = to_low(mm_first(hb_all, all_tokens(dus)))
            hold += (weight_grads["gate"],)
        return hold

    dh = dy + round_the_ring(dz, backward, R, lambda t: (dh_parts[t],), weight_grad)

    grad_again = jnp.sum(dh * ahat, axis=0)
    scaled = dh * again
    da = to_low(ainv * (scaled - ahat * jnp.mean(scaled * ahat, axis=-1, keepdims=True)))
    gate_up_grad = jnp.concatenate([weight_grads["gate"], after(weight_grads["up"], da)], axis=1)
    da_all, _ = gather_tokens(da, (), (gate_up_grad, weight_grads["down_share"]))
    do = to_low(mm_last(da_all, out_w))
    gate_up_share = lax.psum_scatter(after(gate_up_grad, da_all), "shard", scatter_dimension=0, tiled=True)
    dq, dk, dv, products = attend_back(q, k, v, do, place, where)
    down_back = after(exchange(part_down(after(weight_grads["down_share"], da_all)), "rep"), dv)
    products = after(products, down_back)
    out_grad = to_low(mm_first(o, after(da_all, products)))
    out_share = lax.psum_scatter(out_grad, "rep", scatter_dimension=1, tiled=True)
    means = (sum_rows(products) / width).T
    dqkv, head_grads = rope_back(raw, dq, dk, dv, inv, means, head_gains, turn)
    if by_ring:
        head_grads = reverse_pick(head_grads, chip)
    grad_down = collect_down(down_back)
    dqkv = after(dqkv, grad_down)
    grad_down = grad_down.astype(F32)
    late = {}
    qkv_grad = to_low(mm_first(x_all, dqkv))

    def qkv_part(t, hold):
        return qkv_grad[:, t * 3 * HEAD_DIM : (t + 1) * 3 * HEAD_DIM]

    def input_grad(i, hold=None):
        if i == 0:
            dx_all = mm_last(after(dqkv, hold), qkv_w)
            late["keep"], late["send"] = dx_all[:rows], to_low(dx_all[rows:])
            late["gains"] = gain_shares(head_grads, s)
            return (late["keep"], late["send"], late["gains"], gate_up_share, out_grad)
        if i == 2:
            late["hold"] = (hold,)
        return ()

    def gain_shares(head_grads, s):
        wide = jnp.stack([grad_again, grad_mgain]).reshape(2, S, own_width).transpose(1, 0, 2)
        if heads != S:
            head_grads = collect_heads(head_grads, s)
            wide = jnp.sum(exchange(wide, "shard"), axis=0)
        else:
            got = exchange(jnp.concatenate([head_grads, wide], axis=2), "shard")
            head_grads, wide = got[..., :HEAD_DIM], jnp.sum(got[..., HEAD_DIM:], axis=0)
        return jnp.concatenate([head_grads.transpose(1, 0, 2).reshape(2, own_width), wide])

    if by_ring:
        qkv_share = to_low(scatter_pairs(qkv_part, R, input_grad))
    else:
        parts = jnp.concatenate([qkv_part(t, None) for t in range(heads)])
        qkv_share = lax.psum_scatter(parts, "rep", scatter_dimension=0, tiled=True)
        input_grad(0, dqkv)
    dx = dh + by_core(scatter_tokens(late["keep"], late["send"], late.get("hold", ()), (qkv_share,)))

    grad_out = collect_heads(after(out_share, qkv_share).reshape(heads, HEAD_DIM, -1), s)
    grad_out = grad_out.reshape(w_out.shape).astype(F32)
    slots = qkv_share.reshape(per, own_width, 3 * HEAD_DIM)
    back = jnp.stack([permute(pick(slots, (s - k) % per), flip(heads_perm(S, R, per, k))) for k in range(per)])
    back = roll_pick(back, -(s % per)).reshape(per, own_width, 3, HEAD_DIM)
    back = back.transpose(2, 1, 0, 3).reshape(3, own_width, per * HEAD_DIM).astype(F32)

    gain_grads = sum_rep(after(late["gains"], qkv_share))
    gate_up_share = gate_up_share.astype(F32)

    return (
        output,
        dx.reshape(tokens.shape),
        back[0],
        back[1],
        back[2],
        grad_out,
        gain_grads[0],
        gain_grads[1],
        gain_grads[2],
        gate_up_share[:, :ff],
        gate_up_share[:, ff:],
        grad_down,
        gain_grads[3],
    )


def solution(mesh):
    grid = P("shard", "rep")
    rows = P("rep", "shard", None)
    gain = P("shard")
    in_specs = (rows, P("rep"), P("rep", "shard"), grid, grid, grid, grid, gain, gain, gain, grid, grid, grid, gain, rows)
    out_specs = (rows, rows, grid, grid, grid, grid, gain, gain, gain, grid, grid, grid, gain)
    return jax.shard_map(body, mesh=mesh, in_specs=in_specs, out_specs=out_specs, check_vma=False)
```

```python
import jax
import jax.numpy as jnp
from jax import lax
from jax.experimental import pallas as pl
from jax.experimental.pallas import tpu as pltpu
from jax.sharding import PartitionSpec as P

HEADS = 16
HEAD_DIM = 128
PIECE = 256
SCALE = HEAD_DIM ** (-0.5)

LOG2_E = 1.4426950408889634
VMEM = 24 << 20
WIDE_VMEM = 56 << 20

epsilon = 1e-06
rope_base = 500000.0

F32 = jnp.float32
BF16 = jnp.bfloat16

SQUARE = ((0, 0), (0, 2), (1, 0), (1, 1), (0, 1), (0, 3), (1, 2), (1, 3))


def token_order(count):
    return SQUARE if count == 4 else tuple((0, j) for j in range(count))


def to_low(tensor):
    return tensor.astype(BF16)


def dot(left, right, contract):
    return lax.dot_general(left, right, ((contract[0], contract[1]), ((), ())), preferred_element_type=F32)


def mm(left, right):
    return dot(left, right, ((1,), (0,)))


def mm_first(left, right):
    return dot(left, right, ((0,), (0,)))


def mm_last(left, right):
    return dot(left, right, ((1,), (1,)))


def after(value, *others):
    return lax.optimization_barrier((value,) + others)[0]


def send_shard(value, k):
    count = lax.axis_size("shard")
    return lax.ppermute(value, "shard", [(s, s ^ k) for s in range(count)])


def gather_tokens(own, first_hold=(), last_hold=()):
    count = lax.axis_size("shard")
    if count != 4:
        others = [send_shard(own, k) for k in range(1, count)]
        return jnp.concatenate([own] + others), others[0]
    half = own.shape[0] // 2
    a0, b0 = own[:half], own[half:]
    a2 = send_shard(a0, 2)
    b1 = send_shard(b0, 1)
    if first_hold:
        a2, b1 = after(a2, *first_hold), after(b1, *first_hold)
    a02 = jnp.concatenate([a0, a2])
    b01 = jnp.concatenate([b0, b1])
    a13 = send_shard(a02, 1)
    b23 = send_shard(b01, 2)
    last = a13
    if last_hold:
        a13, b23 = after(a13, *last_hold), after(b23, *last_hold)
    return jnp.concatenate([a02, b01, a13, b23]), last


def scatter_tokens(keep, send, first_hold=(), last_hold=()):
    count = lax.axis_size("shard")
    if count != 4:
        parts = jnp.split(jnp.concatenate([keep, send]), count)
        return parts[0] + sum(send_shard(to_low(parts[k]), k).astype(F32) for k in range(1, count))
    q = keep.shape[0] // 2
    send_low = to_low(send)
    a_in = send_shard(send_low[:q], 1)
    b_in = send_shard(send_low[q:], 2)
    if first_hold:
        a_in, b_in = after(a_in, *first_hold), after(b_in, *first_hold)
    a02 = keep[:q] + a_in.astype(F32)
    b01 = keep[q:] + b_in.astype(F32)
    h = q // 2
    a_last = send_shard(to_low(a02[h:]), 2)
    b_last = send_shard(to_low(b01[h:]), 1)
    if last_hold:
        a_last, b_last = after(a_last, *last_hold), after(b_last, *last_hold)
    return jnp.concatenate([a02[:h] + a_last.astype(F32), b01[:h] + b_last.astype(F32)])


def swap_blocks(rows, k):
    order = token_order(lax.axis_size("shard"))
    step = rows.shape[-1] // len(order)
    index = [order.index((h, j ^ k)) for h, j in order]
    return jnp.concatenate([rows[..., i * step : (i + 1) * step] for i in index], axis=-1)


def sum_rows(rows):
    return rows + sum(swap_blocks(send_shard(rows, k), k) for k in range(1, lax.axis_size("shard")))


def unrelative(blocks, s):
    shape = blocks.shape
    bits = shape[0].bit_length() - 1
    cube = blocks.reshape((2,) * bits + shape[1:])
    for bit in range(bits):
        cube = jnp.where((s >> bit) % 2 == 1, jnp.flip(cube, bits - 1 - bit), cube)
    return cube.reshape(shape)


def exchange(blocks, axis):
    return lax.all_to_all(blocks, axis, 0, 0, tiled=True)


def rows_perm(count, heads, k):
    c = count // heads
    return [(s, heads * (s % c) + (s // c + k) % heads) for s in range(count)]


def spread_heads(blocks, s):
    heads, count = blocks.shape[0], lax.axis_size("shard")
    if heads == count:
        return exchange(blocks, "shard")
    q = s // (count // heads)
    got = [lax.ppermute(pick(blocks, (q + k) % heads), "shard", rows_perm(count, heads, k)) for k in range(heads)]
    return reverse_pick(jnp.stack(got), s % heads)


def collect_heads(blocks, s):
    heads, count = blocks.shape[0], lax.axis_size("shard")
    if heads == count:
        return exchange(blocks, "shard")
    q = s // (count // heads)
    got = [
        lax.ppermute(pick(blocks, (s - k) % heads), "shard", flip(rows_perm(count, heads, k))) for k in range(heads)
    ]
    return roll_pick(jnp.stack(got), -q)


def ring(value, count):
    return lax.ppermute(value, "rep", [(r, (r + 2) % count) for r in range(count)])


def sibling(value, count):
    return lax.ppermute(value, "rep", [(r, r ^ 1) for r in range(count)])


def gather_pairs(own, count):
    blocks = [own]
    for _ in range(count // 2 - 1):
        blocks.append(ring(blocks[-1], count))
    pairs = []
    for i, block in enumerate(blocks):
        other = sibling(block, count)
        pairs.append((block, after(other, blocks[i + 1]) if i + 1 < len(blocks) else other))
    return pairs


def scatter_pairs(part_of, count, beside=lambda i, low: ()):
    total = low = None
    for i, step in enumerate(list(range(1, count // 2)) + [0]):
        part = part_of(step, low)
        half = part.shape[0] // 2
        mine = part[:half].astype(F32) + sibling(to_low(part[half:]), count).astype(F32)
        if total is None:
            total = mine
        else:
            got = ring(low, count)
            hold = beside(i - 1, low)
            if hold:
                got = after(got, *hold)
            total = got.astype(F32) + mine
        low = to_low(total)
    return total


def round_the_ring(own, compute, count, early, late, own_last=False):
    chips = count // 2

    def mine(part):
        middle = part.shape[0] // 2
        return part[:middle] + sibling(to_low(part[middle:]), count).astype(F32)

    block, parts, total = own, [], None
    for t in range(chips):
        following = ring(block, count) if t + 1 < chips else None
        pair = jnp.concatenate([block, sibling(block, count)])
        if t == 0 and own_last:
            own_pair = pair
        parts.append(compute(t, pair) if t or not own_last else None)
        if t == 1:
            total = mine(parts[1])
        if following is not None:
            hold = early(t) + ((to_low(total),) if t == chips - 2 else ())
            block = after(following, *hold) if hold else following
    for step, t in enumerate(list(range(2, chips)) + [0]):
        low = to_low(total)
        got = ring(low, count)
        if parts[0] is None and step == 1:
            parts[0] = compute(0, after(own_pair, low))
        hold = late(step, low)
        if hold:
            got = after(got, *hold)
        total = got.astype(F32) + mine(parts[t])
    return total


def heads_perm(shard_count, rep_count, per, k):
    group = shard_count // per
    pairs = []
    for r in range(rep_count):
        for s in range(shard_count):
            j = (s % per + k) % per
            target = (r // group * group + s // per, per * (r % group) + j)
            pairs.append((r * shard_count + s, target[0] * shard_count + target[1]))
    return pairs


def flip_rep(value, d):
    count = lax.axis_size("rep")
    return lax.ppermute(value, "rep", [(i, i ^ d) for i in range(count)])


def sum_rep(value):
    d = 1
    while d < lax.axis_size("rep"):
        value = value + flip_rep(value, d)
        d *= 2
    return value


def spread_down(rows):
    S, R = lax.axis_size("shard"), lax.axis_size("rep")
    share, columns = rows.shape[0] // R, rows.shape[1]
    units = rows.reshape(R // S, S, share, columns).transpose(1, 0, 2, 3)
    return exchange(units, "shard").reshape(R, share, columns)


def join_down(pieces):
    R, share, columns = pieces.shape
    return pieces.transpose(1, 0, 2).reshape(share, R * columns)


def part_down(rows):
    share, R = rows.shape[0], lax.axis_size("rep")
    return rows.reshape(share, R, -1).transpose(1, 0, 2)


def collect_down(pieces):
    R, share, columns = pieces.shape
    S = lax.axis_size("shard")
    units = exchange(pieces.reshape(S, R // S, share, columns), "shard")
    return units.transpose(1, 0, 2, 3).reshape(R * share, columns)


def flip(pairs):
    return [(b, a) for a, b in pairs]


def permute(value, pairs):
    return lax.ppermute(value, ("rep", "shard"), pairs)


def pick(values, index):
    return lax.dynamic_index_in_dim(values, index, 0, keepdims=False)


def roll_pick(values, shift):
    n = values.shape[0]
    if n == 1:
        return values
    return lax.dynamic_slice_in_dim(jnp.concatenate([values, values]), shift % n, n, 0)


def reverse_pick(values, base):
    n = values.shape[0]
    if n == 1:
        return values
    return roll_pick(values[::-1], n - 1 - base)


def frequencies():
    return jnp.power(jnp.float32(rope_base), -2.0 * jnp.arange(HEAD_DIM // 2, dtype=F32) / HEAD_DIM)


def bias_of(piece_first, row, col):
    row_in = (row >= piece_first) & (row < piece_first + PIECE)
    col_in = (col >= piece_first) & (col < piece_first + PIECE)
    return jnp.where((col <= row) | (row_in & col_in), 0.0, -1e30).astype(F32)


def attend_kernel(where_ref, q_ref, k_ref, v_ref, row_ref, col_ref, o_ref, bias_ref):
    @pl.when(pl.program_id(1) == 0)
    def _():
        bias_ref[...] = bias_of(where_ref[where_ref.shape[0] - 1], row_ref[...], col_ref[...])

    scores = mm_last(q_ref[0], k_ref[0]) * (SCALE * LOG2_E) + bias_ref[...]
    powers = jnp.exp2(scores - jnp.max(scores, axis=-1, keepdims=True))
    weights = powers * (1.0 / jnp.sum(powers, axis=-1, keepdims=True))
    o_ref[...] = to_low(mm(to_low(weights), v_ref[0]))


def attend(q, k, v, place, where, block=256):
    heads, n, hd = q.shape
    whole = pl.BlockSpec((1, n, hd), lambda b, t, w: (t, 0, 0))
    return pl.pallas_call(
        attend_kernel,
        out_shape=jax.ShapeDtypeStruct((n, heads * hd), BF16),
        grid_spec=pltpu.PrefetchScalarGridSpec(
            num_scalar_prefetch=1,
            grid=(n // block, heads),
            in_specs=[
                pl.BlockSpec((1, block, hd), lambda b, t, w: (t, b, 0)),
                whole,
                whole,
                pl.BlockSpec((block, 1), lambda b, t, w: (b, 0)),
                pl.BlockSpec((1, n), lambda b, t, w: (0, 0)),
            ],
            out_specs=pl.BlockSpec((block, hd), lambda b, t, w: (b, w[t])),
            scratch_shapes=[pltpu.VMEM((block, n), F32)],
        ),
        compiler_params=pltpu.CompilerParams(vmem_limit_bytes=VMEM),
        cost_estimate=pl.CostEstimate(
            flops=4 * heads * n * n * hd, bytes_accessed=8 * heads * n * hd, transcendentals=heads * n * n
        ),
        name="attend",
    )(where, q, k, v, place[:, None], place[None, :])


def attend_back_kernel(where_ref, q_ref, k_ref, v_ref, do_ref, row_ref, col_ref, dq_ref, dk_ref, dv_ref, products_ref, bias_ref):
    t, b = pl.program_id(0), pl.program_id(1)

    @pl.when(pl.program_id(0) == 0)
    def _():
        bias_ref[b] = bias_of(where_ref[where_ref.shape[0] - 1], row_ref[...], col_ref[...])

    q, k, v, do = q_ref[0], k_ref[0], v_ref[0], do_ref[...]
    scores = mm_last(k, q) * (SCALE * LOG2_E) + bias_ref[b]
    powers = jnp.exp2(scores - jnp.max(scores, axis=0, keepdims=True))
    probs = powers * (1.0 / jnp.sum(powers, axis=0, keepdims=True))
    grad_probs = mm_last(v, do)
    delta = jnp.sum(probs * grad_probs, axis=0, keepdims=True)
    grad_scores = to_low(probs * (grad_probs - delta))
    dq = mm_first(grad_scores, k) * SCALE
    dq_ref[0] = dq
    dk = mm(grad_scores, q) * SCALE
    dv = mm(to_low(probs), do)

    @pl.when((t == 0) & (b == 0))
    def _():
        products_ref[...] = jnp.zeros_like(products_ref)

    own = pl.ds(pl.multiple_of(b * q.shape[0], q.shape[0]), q.shape[0])
    products_ref[0:1, own] += jnp.sum((dq * q.astype(F32)).T, axis=0, keepdims=True)

    @pl.when(b == 0)
    def _():
        dk_ref[0] = dk
        dv_ref[0] = dv

    @pl.when(b > 0)
    def _():
        dk_ref[0] += dk
        dv_ref[0] += dv

    @pl.when(b == pl.num_programs(1) - 1)
    def _():
        products_ref[1:2, :] += jnp.sum((dk_ref[0] * k.astype(F32)).T, axis=0, keepdims=True)


def attend_back(q, k, v, do, place, where, block=512):
    heads, n, hd = q.shape
    one = pl.BlockSpec((1, block, hd), lambda t, b, w: (t, b, 0))
    whole = pl.BlockSpec((1, n, hd), lambda t, b, w: (t, 0, 0))
    return pl.pallas_call(
        attend_back_kernel,
        out_shape=[jax.ShapeDtypeStruct((heads, n, hd), F32)] * 3 + [jax.ShapeDtypeStruct((2, n), F32)],
        grid_spec=pltpu.PrefetchScalarGridSpec(
            num_scalar_prefetch=1,
            grid=(heads, n // block),
            in_specs=[
                one,
                whole,
                whole,
                pl.BlockSpec((block, hd), lambda t, b, w: (b, w[t])),
                pl.BlockSpec((1, block), lambda t, b, w: (0, b)),
                pl.BlockSpec((n, 1), lambda t, b, w: (0, 0)),
            ],
            out_specs=[one, whole, whole, pl.BlockSpec((2, n), lambda t, b, w: (0, 0))],
            scratch_shapes=[pltpu.VMEM((n // block, n, block), F32)],
        ),
        compiler_params=pltpu.CompilerParams(vmem_limit_bytes=32 << 20),
        cost_estimate=pl.CostEstimate(
            flops=10 * heads * n * n * hd, bytes_accessed=20 * heads * n * hd, transcendentals=heads * n * n
        ),
        name="attend_back",
    )(where, q, k, v, do, place[None, :], place[:, None])


def columns_of(t, i):
    return slice((3 * t + i) * HEAD_DIM, (3 * t + i + 1) * HEAD_DIM)


def squares_kernel(heads, raw_ref, out_ref):
    for i in (0, 1):
        total = sum(jnp.square(raw_ref[:, columns_of(t, i)]) for t in range(heads))
        out_ref[i : i + 1, :] = jnp.sum(total.T, axis=0, keepdims=True)


def squares(raw, heads, block=256):
    n, width = raw.shape
    return pl.pallas_call(
        lambda *refs: squares_kernel(heads, *refs),
        out_shape=jax.ShapeDtypeStruct((2, n), F32),
        grid=(n // block,),
        in_specs=[pl.BlockSpec((block, width), lambda b: (b, 0))],
        out_specs=pl.BlockSpec((2, block), lambda b: (0, b)),
        compiler_params=pltpu.CompilerParams(vmem_limit_bytes=VMEM),
        cost_estimate=pl.CostEstimate(flops=heads * n * 512, bytes_accessed=heads * n * 1536, transcendentals=0),
        name="squares",
    )(raw)


def turn_half(tensor):
    return pltpu.roll(tensor, HEAD_DIM // 2, 1)


def rope_kernel(heads, raw_ref, inv_ref, gain_ref, turn_ref, q_ref, k_ref, v_ref):
    cosines, sines = turn_ref[:, :HEAD_DIM], turn_ref[:, HEAD_DIM:]
    for t in range(heads):
        for i, out in enumerate((q_ref, k_ref)):
            value = raw_ref[:, columns_of(t, i)] * inv_ref[:, i : i + 1] * gain_ref[t, i : i + 1, :]
            out[t] = to_low(value * cosines + turn_half(value) * sines)
        v_ref[t] = to_low(raw_ref[:, columns_of(t, 2)])


def rope(raw, inv, gain, turn, block=256):
    heads, n = gain.shape[0], raw.shape[0]
    rows = lambda width: pl.BlockSpec((block, width), lambda b: (b, 0))
    out = pl.BlockSpec((heads, block, HEAD_DIM), lambda b: (0, b, 0))
    return pl.pallas_call(
        lambda *refs: rope_kernel(heads, *refs),
        out_shape=[jax.ShapeDtypeStruct((heads, n, HEAD_DIM), BF16)] * 3,
        grid=(n // block,),
        in_specs=[
            rows(raw.shape[1]),
            rows(2),
            pl.BlockSpec((heads, 2, HEAD_DIM), lambda b: (0, 0, 0)),
            rows(2 * HEAD_DIM),
        ],
        out_specs=[out] * 3,
        compiler_params=pltpu.CompilerParams(vmem_limit_bytes=VMEM),
        cost_estimate=pl.CostEstimate(flops=heads * n * 2000, bytes_accessed=heads * n * 2304, transcendentals=0),
        name="rope",
    )(raw, inv, gain, turn)


def rope_back_kernel(
    heads, raw_ref, dq_ref, dk_ref, dv_ref, inv_ref, mean_ref, gain_ref, turn_ref, out_ref, grad_ref
):
    @pl.when(pl.program_id(0) == 0)
    def _():
        grad_ref[...] = jnp.zeros_like(grad_ref)

    cosines, sines = turn_ref[:, :HEAD_DIM], turn_ref[:, HEAD_DIM:]
    for t in range(heads):
        for i, grad in enumerate((dq_ref, dk_ref)):
            inv = inv_ref[:, i : i + 1]
            hat = raw_ref[:, columns_of(t, i)] * inv
            back = grad[t] * cosines - turn_half(grad[t]) * sines
            grad_ref[t, i : i + 1, :] += jnp.sum(back * hat, axis=0, keepdims=True)
            row = inv * (back * gain_ref[t, i : i + 1, :] - hat * mean_ref[:, i : i + 1])
            out_ref[:, columns_of(t, i)] = to_low(row)
        out_ref[:, columns_of(t, 2)] = to_low(dv_ref[t])


def rope_back(raw, dq, dk, dv, inv, mean, gain, turn, block=256):
    heads, (n, width) = gain.shape[0], raw.shape
    rows = lambda width: pl.BlockSpec((block, width), lambda b: (b, 0))
    grad = pl.BlockSpec((heads, block, HEAD_DIM), lambda b: (0, b, 0))
    gains = pl.BlockSpec((heads, 2, HEAD_DIM), lambda b: (0, 0, 0))
    return pl.pallas_call(
        lambda *refs: rope_back_kernel(heads, *refs),
        out_shape=[jax.ShapeDtypeStruct((n, width), BF16), jax.ShapeDtypeStruct((heads, 2, HEAD_DIM), F32)],
        grid=(n // block,),
        in_specs=[rows(width)] + [grad] * 3 + [rows(2), rows(2), gains, rows(2 * HEAD_DIM)],
        out_specs=[rows(width), gains],
        compiler_params=pltpu.CompilerParams(vmem_limit_bytes=WIDE_VMEM),
        cost_estimate=pl.CostEstimate(flops=heads * n * 4000, bytes_accessed=heads * n * 3840, transcendentals=0),
        name="rope_back",
    )(raw, dq, dk, dv, inv, mean, gain, turn)


def body(
    tokens,
    piece_start,
    positions,
    w_query,
    w_key,
    w_value,
    w_out,
    query_gain,
    key_gain,
    attn_gain,
    w_gate,
    w_up,
    w_down,
    mlp_gain,
    cotangent,
):
    S = lax.axis_size("shard")
    R = lax.axis_size("rep")
    s = lax.axis_index("shard")
    r = lax.axis_index("rep")
    _, span, width = tokens.shape
    heads = HEADS // S
    per = HEADS // R
    own_width = width // S
    x_own = tokens.reshape(span, width)

    by_ring = per * 2 == S
    chip, core = r // 2, r % 2

    def head_columns(j):
        start = j * HEAD_DIM
        return jnp.concatenate(
            [to_low(lax.dynamic_slice_in_dim(w, start, HEAD_DIM, 1)) for w in (w_query, w_key, w_value)], axis=1
        )

    def by_core(value):
        if not by_ring:
            return value
        middle = value.shape[1] // 2
        return jnp.where(core == 1, jnp.concatenate([value[:, middle:], value[:, :middle]], axis=1), value)

    own_columns = [head_columns((s + k) % per) for k in range(per)]
    got = [permute(value, heads_perm(S, R, per, k)) for k, value in enumerate(own_columns)]
    gains_own = jnp.stack([to_low(g).astype(F32) for g in (query_gain, key_gain, attn_gain, mlp_gain)])
    small = jnp.concatenate([positions.reshape(span).astype(F32), gains_own.reshape(-1)])
    small_all = [small] + [send_shard(small, k) for k in range(1, S)]
    own_out = spread_heads(after(to_low(w_out), *own_columns).reshape(heads, HEAD_DIM, -1), s)
    got, small_all, own_out = lax.optimization_barrier((got, small_all, own_out))

    got = reverse_pick(jnp.stack(got), s % per).reshape(per * own_width, 3 * HEAD_DIM)
    if by_ring:
        qkv_pairs = gather_pairs(got, R)
        qkv_w = jnp.zeros((width, heads * 3 * HEAD_DIM), BF16)
        for t, pair in enumerate(qkv_pairs):
            for i, block in enumerate(pair):
                qkv_w = lax.dynamic_update_slice(qkv_w, block, (i * block.shape[0], t * block.shape[1]))
        head_order = (chip - jnp.arange(heads)) % heads
        ring_start, ring_late, ring_end = qkv_pairs[1][0], qkv_pairs[-2][0], qkv_pairs[-1][0]
    else:
        qkv_w = lax.all_gather(got, "rep", axis=0, tiled=True).reshape(heads, width, 3 * HEAD_DIM)
        qkv_w = jnp.concatenate(list(qkv_w), axis=1)
        head_order = jnp.arange(heads)
        ring_start = ring_late = ring_end = qkv_w
    where = jnp.concatenate([head_order, piece_start]).astype(jnp.int32)
    x_all, x_last = gather_tokens(by_core(after(x_own, got)), (ring_start,), (ring_late,))
    gate_up = after(jnp.concatenate([to_low(w_gate), to_low(w_up)], axis=1), x_last)
    gate_up_w = lax.all_gather(gate_up, "shard", axis=0, tiled=True)

    own_out = own_out.reshape(own_width, -1)
    columns = own_out.shape[1]

    gains = unrelative(jnp.stack([v[span:].reshape(4, own_width) for v in small_all]), s)
    gains = gains.transpose(1, 0, 2).reshape(4, width)
    head_gains = gains[:2].reshape(2, heads, S, HEAD_DIM)
    head_gains = lax.dynamic_index_in_dim(head_gains, s, 2, keepdims=False)
    head_gains = head_gains.transpose(1, 0, 2)
    if by_ring:
        head_gains = reverse_pick(head_gains, chip)
    again, mgain = gains[2], gains[3]
    order = token_order(S)
    step = S * span // len(order)
    place_pos = jnp.concatenate([small_all[j][h * step : (h + 1) * step] for h, j in order])
    place = jnp.concatenate([(s ^ j) * span + h * step + lax.iota(jnp.int32, step) for h, j in order])
    angles = place_pos[:, None] * frequencies()
    cosines, sines = jnp.cos(angles), jnp.sin(angles)
    turn = jnp.concatenate([cosines, cosines, -sines, sines], axis=1)

    raw = mm(x_all, qkv_w)
    raw_squares = squares(raw, heads)
    inv = lax.rsqrt(sum_rows(raw_squares) / width + epsilon).T
    q, k, v = rope(raw, inv, head_gains, turn)
    pieces = spread_down(after(to_low(w_down), q))
    o = attend(q, k, v, place, where)

    out_w = jnp.zeros((own_width, width), BF16)
    block = after(own_out, ring_end)
    for t in range(R // 2):
        if t:
            block = after(ring(block, R), (raw_squares, q, o)[min(t - 1, 2)])
        for i, value in enumerate((block, sibling(block, R))):
            start = ((chip - t) % (R // 2) * 2 + (core ^ i)) * columns
            out_w = lax.dynamic_update_slice_in_dim(out_w, value, start, 1)
    rows = S * span // 2
    a_send = mm(o[rows:], out_w)
    a_keep = mm(o[:rows], out_w)
    down_blocks = exchange(after(pieces, a_keep), "rep")
    a = scatter_tokens(a_keep, a_send, (down_blocks,))
    ainv = lax.rsqrt(jnp.mean(a * a, axis=-1, keepdims=True) + epsilon)
    ahat = a * ainv
    h = x_own.astype(F32) + ahat * again
    hb = to_low(h)

    down_w = lax.all_gather(join_down(after(down_blocks, hb)), "shard", axis=0, tiled=True)
    chips, ff = R // 2, w_gate.shape[1]
    kept = {}

    def forward(t, pair):
        gu = mm(pair, gate_up_w)
        g, u = gu[:, :ff], gu[:, ff:]
        inner = to_low(g * jax.nn.sigmoid(g) * u)
        kept[t] = (g, u, inner, pair)
        return mm(inner, down_w)

    z = round_the_ring(hb, forward, R, lambda t: (), lambda step, low: (), True)
    zinv = lax.rsqrt(jnp.mean(z * z, axis=-1, keepdims=True) + epsilon)
    zhat = z * zinv
    output = to_low(h + zhat * mgain).reshape(tokens.shape)

    dy = cotangent.reshape(span, width).astype(F32)
    grad_mgain = jnp.sum(dy * zhat, axis=0)
    scaled = dy * mgain
    dz = to_low(zinv * (scaled - zhat * jnp.mean(scaled * zhat, axis=-1, keepdims=True)))
    dgs, dus, dz_pairs, dh_parts, weight_grads = {}, {}, {}, {}, {}

    def backward(t, pair):
        g, u = kept[t][:2]
        dm = mm_last(pair, down_w)
        sig = jax.nn.sigmoid(g)
        dz_pairs[t] = pair
        dgs[t] = to_low(dm * u * sig * (1.0 + g * (1.0 - sig)))
        dus[t] = to_low(dm * g * sig)
        dh_parts[t] = mm_last(jnp.concatenate([dgs[t], dus[t]], axis=1), gate_up_w)
        return dh_parts[t]

    def all_tokens(values, hold):
        return jnp.concatenate([after(values[t], hold) for t in range(chips)])

    def weight_grad(step, low):
        hold = (dh_parts[chips - 1],) if step == 0 else ()
        if step == chips - 3:
            inner_all = all_tokens({t: kept[t][2] for t in kept}, low)
            down_grad = to_low(mm_first(inner_all, all_tokens(dz_pairs, low)))
            weight_grads["down"] = down_grad
            weight_grads["down_share"] = lax.psum_scatter(down_grad, "shard", scatter_dimension=0, tiled=True)
            hold += (down_grad,)
        if step == chips - 2:
            hb_all = all_tokens({t: kept[t][3] for t in kept}, low)
            weight_grads["gate"] = to_low(mm_first(hb_all, all_tokens(dgs, low)))
            weight_grads["up"] = to_low(mm_first(hb_all, all_tokens(dus, low)))
            hold += (weight_grads["gate"],)
        return hold

    dh = dy + round_the_ring(dz, backward, R, lambda t: (dh_parts[t],), weight_grad)

    grad_again = jnp.sum(dh * ahat, axis=0)
    scaled = dh * again
    da = to_low(ainv * (scaled - ahat * jnp.mean(scaled * ahat, axis=-1, keepdims=True)))
    gate_up_grad = jnp.concatenate([weight_grads["gate"], after(weight_grads["up"], da)], axis=1)
    da_all, _ = gather_tokens(da, (), (gate_up_grad, weight_grads["down_share"]))
    do = to_low(mm_last(da_all, out_w))
    gate_up_share = lax.psum_scatter(after(gate_up_grad, da_all), "shard", scatter_dimension=0, tiled=True)
    dq, dk, dv, products = attend_back(q, k, v, do, place, where)
    down_back = after(exchange(part_down(after(weight_grads["down_share"], da_all)), "rep"), dv)
    products = after(products, down_back)
    means = (sum_rows(products) / width).T
    dqkv, head_grads = rope_back(raw, dq, dk, dv, inv, means, head_gains, turn)
    if by_ring:
        head_grads = reverse_pick(head_grads, chip)
    grad_down = collect_down(down_back)
    dqkv = after(dqkv, grad_down)
    grad_down = grad_down.astype(F32)
    late = {}
    qkv_grad = to_low(mm_first(x_all, dqkv))

    def qkv_part(t, hold):
        return qkv_grad[:, t * 3 * HEAD_DIM : (t + 1) * 3 * HEAD_DIM]

    def input_grad(i, hold=None):
        if i == 0:
            dx_all = mm_last(after(dqkv, hold), qkv_w)
            late["keep"], late["send"] = dx_all[:rows], to_low(dx_all[rows:])
            out_grad = to_low(mm_first(o, after(da_all, hold)))
            late["out"] = lax.psum_scatter(out_grad, "rep", scatter_dimension=1, tiled=True)
            late["gains"] = gain_shares(after(head_grads, hold), s)
            return (late["keep"], late["send"], late["gains"], gate_up_share, out_grad)
        if i == 2:
            late["hold"] = (hold,)
            late["out"] = collect_heads(after(late["out"], hold).reshape(heads, HEAD_DIM, -1), s)
            return (late["out"],)
        return ()

    def gain_shares(head_grads, s):
        wide = jnp.stack([grad_again, grad_mgain]).reshape(2, S, own_width).transpose(1, 0, 2)
        if heads != S:
            head_grads = collect_heads(head_grads, s)
            wide = jnp.sum(exchange(wide, "shard"), axis=0)
        else:
            got = exchange(jnp.concatenate([head_grads, wide], axis=2), "shard")
            head_grads, wide = got[..., :HEAD_DIM], jnp.sum(got[..., HEAD_DIM:], axis=0)
        return jnp.concatenate([head_grads.transpose(1, 0, 2).reshape(2, own_width), wide])

    if by_ring:
        qkv_share = to_low(scatter_pairs(qkv_part, R, input_grad))
    else:
        parts = jnp.concatenate([qkv_part(t, None) for t in range(heads)])
        qkv_share = lax.psum_scatter(parts, "rep", scatter_dimension=0, tiled=True)
        input_grad(0, dqkv)
    dx = dh + by_core(scatter_tokens(late["keep"], late["send"], late.get("hold", ()), (qkv_share,)))

    if not by_ring:
        late["out"] = collect_heads(late["out"].reshape(heads, HEAD_DIM, -1), s)
    grad_out = late["out"].reshape(w_out.shape).astype(F32)
    slots = qkv_share.reshape(per, own_width, 3 * HEAD_DIM)
    back = jnp.stack([permute(pick(slots, (s - k) % per), flip(heads_perm(S, R, per, k))) for k in range(per)])
    back = roll_pick(back, -(s % per)).reshape(per, own_width, 3, HEAD_DIM)
    back = back.transpose(2, 1, 0, 3).reshape(3, own_width, per * HEAD_DIM).astype(F32)

    gain_grads = sum_rep(after(late["gains"], qkv_share))
    gate_up_share = gate_up_share.astype(F32)

    return (
        output,
        dx.reshape(tokens.shape),
        back[0],
        back[1],
        back[2],
        grad_out,
        gain_grads[0],
        gain_grads[1],
        gain_grads[2],
        gate_up_share[:, :ff],
        gate_up_share[:, ff:],
        grad_down,
        gain_grads[3],
    )


def solution(mesh):
    grid = P("shard", "rep")
    rows = P("rep", "shard", None)
    gain = P("shard")
    in_specs = (rows, P("rep"), P("rep", "shard"), grid, grid, grid, grid, gain, gain, gain, grid, grid, grid, gain, rows)
    out_specs = (rows, rows, grid, grid, grid, grid, gain, gain, gain, grid, grid, grid, gain)
    return jax.shard_map(body, mesh=mesh, in_specs=in_specs, out_specs=out_specs, check_vma=False)
```

```python
import jax
import jax.numpy as jnp
from jax import lax
from jax.experimental import pallas as pl
from jax.experimental.pallas import tpu as pltpu
from jax.sharding import PartitionSpec as P

HEADS = 16
HEAD_DIM = 128
PIECE = 256
SCALE = HEAD_DIM ** (-0.5)

LOG2_E = 1.4426950408889634
VMEM = 24 << 20
WIDE_VMEM = 56 << 20

epsilon = 1e-06
rope_base = 500000.0

F32 = jnp.float32
BF16 = jnp.bfloat16

SQUARE = ((0, 0), (0, 2), (1, 0), (1, 1), (0, 1), (0, 3), (1, 2), (1, 3))


def token_order(count):
    return SQUARE if count == 4 else tuple((0, j) for j in range(count))


def to_low(tensor):
    return tensor.astype(BF16)


def dot(left, right, contract):
    return lax.dot_general(left, right, ((contract[0], contract[1]), ((), ())), preferred_element_type=F32)


def mm(left, right):
    return dot(left, right, ((1,), (0,)))


def mm_first(left, right):
    return dot(left, right, ((0,), (0,)))


def mm_last(left, right):
    return dot(left, right, ((1,), (1,)))


def after(value, *others):
    return lax.optimization_barrier((value,) + others)[0]


def send_shard(value, k):
    count = lax.axis_size("shard")
    return lax.ppermute(value, "shard", [(s, s ^ k) for s in range(count)])


def gather_tokens(own, first_hold=(), last_hold=()):
    count = lax.axis_size("shard")
    if count != 4:
        others = [send_shard(own, k) for k in range(1, count)]
        return jnp.concatenate([own] + others), others[0]
    half = own.shape[0] // 2
    a0, b0 = own[:half], own[half:]
    a2 = send_shard(a0, 2)
    b1 = send_shard(b0, 1)
    if first_hold:
        a2, b1 = after(a2, *first_hold), after(b1, *first_hold)
    a02 = jnp.concatenate([a0, a2])
    b01 = jnp.concatenate([b0, b1])
    a13 = send_shard(a02, 1)
    b23 = send_shard(b01, 2)
    last = a13
    if last_hold:
        a13, b23 = after(a13, *last_hold), after(b23, *last_hold)
    return jnp.concatenate([a02, b01, a13, b23]), last


def scatter_tokens(keep, send, first_hold=(), last_hold=()):
    count = lax.axis_size("shard")
    if count != 4:
        parts = jnp.split(jnp.concatenate([keep, send]), count)
        return parts[0] + sum(send_shard(to_low(parts[k]), k).astype(F32) for k in range(1, count))
    q = keep.shape[0] // 2
    send_low = to_low(send)
    a_in = send_shard(send_low[:q], 1)
    b_in = send_shard(send_low[q:], 2)
    if first_hold:
        a_in, b_in = after(a_in, *first_hold), after(b_in, *first_hold)
    a02 = keep[:q] + a_in.astype(F32)
    b01 = keep[q:] + b_in.astype(F32)
    h = q // 2
    a_last = send_shard(to_low(a02[h:]), 2)
    b_last = send_shard(to_low(b01[h:]), 1)
    if last_hold:
        a_last, b_last = after(a_last, *last_hold), after(b_last, *last_hold)
    return jnp.concatenate([a02[:h] + a_last.astype(F32), b01[:h] + b_last.astype(F32)])


def swap_blocks(rows, k):
    order = token_order(lax.axis_size("shard"))
    step = rows.shape[-1] // len(order)
    index = [order.index((h, j ^ k)) for h, j in order]
    return jnp.concatenate([rows[..., i * step : (i + 1) * step] for i in index], axis=-1)


def sum_rows(rows):
    return rows + sum(swap_blocks(send_shard(rows, k), k) for k in range(1, lax.axis_size("shard")))


def unrelative(blocks, s):
    shape = blocks.shape
    bits = shape[0].bit_length() - 1
    cube = blocks.reshape((2,) * bits + shape[1:])
    for bit in range(bits):
        cube = jnp.where((s >> bit) % 2 == 1, jnp.flip(cube, bits - 1 - bit), cube)
    return cube.reshape(shape)


def exchange(blocks, axis):
    return lax.all_to_all(blocks, axis, 0, 0, tiled=True)


def rows_perm(count, heads, k):
    c = count // heads
    return [(s, heads * (s % c) + (s // c + k) % heads) for s in range(count)]


def spread_heads(blocks, s):
    heads, count = blocks.shape[0], lax.axis_size("shard")
    if heads == count:
        return exchange(blocks, "shard")
    q = s // (count // heads)
    got = [lax.ppermute(pick(blocks, (q + k) % heads), "shard", rows_perm(count, heads, k)) for k in range(heads)]
    return reverse_pick(jnp.stack(got), s % heads)


def collect_heads(blocks, s):
    heads, count = blocks.shape[0], lax.axis_size("shard")
    if heads == count:
        return exchange(blocks, "shard")
    q = s // (count // heads)
    got = [
        lax.ppermute(pick(blocks, (s - k) % heads), "shard", flip(rows_perm(count, heads, k))) for k in range(heads)
    ]
    return roll_pick(jnp.stack(got), -q)


def ring(value, count):
    return lax.ppermute(value, "rep", [(r, (r + 2) % count) for r in range(count)])


def sibling(value, count):
    return lax.ppermute(value, "rep", [(r, r ^ 1) for r in range(count)])


def gather_pairs(own, count):
    blocks = [own]
    for _ in range(count // 2 - 1):
        blocks.append(ring(blocks[-1], count))
    pairs = []
    for i, block in enumerate(blocks):
        other = sibling(block, count)
        pairs.append((block, after(other, blocks[i + 1]) if i + 1 < len(blocks) else other))
    return pairs


def scatter_pairs(part_of, count, beside=lambda i, low: ()):
    total = low = None
    for i, step in enumerate(list(range(1, count // 2)) + [0]):
        part = part_of(step, low)
        half = part.shape[0] // 2
        mine = part[:half].astype(F32) + sibling(to_low(part[half:]), count).astype(F32)
        if total is None:
            total = mine
        else:
            got = ring(low, count)
            hold = beside(i - 1, low)
            if hold:
                got = after(got, *hold)
            total = got.astype(F32) + mine
        low = to_low(total)
    return total


def round_the_ring(own, compute, count, early, late, own_last=False):
    chips = count // 2

    def mine(part):
        middle = part.shape[0] // 2
        return part[:middle] + sibling(to_low(part[middle:]), count).astype(F32)

    block, parts, total = own, [], None
    for t in range(chips):
        following = ring(block, count) if t + 1 < chips else None
        pair = jnp.concatenate([block, sibling(block, count)])
        if t == 0 and own_last:
            own_pair = pair
        parts.append(compute(t, pair) if t or not own_last else None)
        if t == 1:
            total = mine(parts[1])
        if following is not None:
            hold = early(t) + ((to_low(total),) if t == chips - 2 else ())
            block = after(following, *hold) if hold else following
    for step, t in enumerate(list(range(2, chips)) + [0]):
        low = to_low(total)
        got = ring(low, count)
        if parts[0] is None and step == 1:
            parts[0] = compute(0, after(own_pair, low))
        hold = late(step, low)
        if hold:
            got = after(got, *hold)
        total = got.astype(F32) + mine(parts[t])
    return total


def heads_perm(shard_count, rep_count, per, k):
    group = shard_count // per
    pairs = []
    for r in range(rep_count):
        for s in range(shard_count):
            j = (s % per + k) % per
            target = (r // group * group + s // per, per * (r % group) + j)
            pairs.append((r * shard_count + s, target[0] * shard_count + target[1]))
    return pairs


def flip_rep(value, d):
    count = lax.axis_size("rep")
    return lax.ppermute(value, "rep", [(i, i ^ d) for i in range(count)])


def sum_rep(value):
    d = 1
    while d < lax.axis_size("rep"):
        value = value + flip_rep(value, d)
        d *= 2
    return value


def spread_down(rows):
    S, R = lax.axis_size("shard"), lax.axis_size("rep")
    share, columns = rows.shape[0] // R, rows.shape[1]
    units = rows.reshape(R // S, S, share, columns).transpose(1, 0, 2, 3)
    return exchange(units, "shard").reshape(R, share, columns)


def join_down(pieces):
    R, share, columns = pieces.shape
    return pieces.transpose(1, 0, 2).reshape(share, R * columns)


def part_down(rows):
    share, R = rows.shape[0], lax.axis_size("rep")
    return rows.reshape(share, R, -1).transpose(1, 0, 2)


def collect_down(pieces):
    R, share, columns = pieces.shape
    S = lax.axis_size("shard")
    units = exchange(pieces.reshape(S, R // S, share, columns), "shard")
    return units.transpose(1, 0, 2, 3).reshape(R * share, columns)


def flip(pairs):
    return [(b, a) for a, b in pairs]


def permute(value, pairs):
    return lax.ppermute(value, ("rep", "shard"), pairs)


def pick(values, index):
    return lax.dynamic_index_in_dim(values, index, 0, keepdims=False)


def roll_pick(values, shift):
    n = values.shape[0]
    if n == 1:
        return values
    return lax.dynamic_slice_in_dim(jnp.concatenate([values, values]), shift % n, n, 0)


def reverse_pick(values, base):
    n = values.shape[0]
    if n == 1:
        return values
    return roll_pick(values[::-1], n - 1 - base)


def frequencies():
    return jnp.power(jnp.float32(rope_base), -2.0 * jnp.arange(HEAD_DIM // 2, dtype=F32) / HEAD_DIM)


def bias_of(piece_first, row, col):
    row_in = (row >= piece_first) & (row < piece_first + PIECE)
    col_in = (col >= piece_first) & (col < piece_first + PIECE)
    return jnp.where((col <= row) | (row_in & col_in), 0.0, -1e30).astype(F32)


def attend_kernel(where_ref, q_ref, k_ref, v_ref, row_ref, col_ref, o_ref, bias_ref):
    @pl.when(pl.program_id(1) == 0)
    def _():
        bias_ref[...] = bias_of(where_ref[where_ref.shape[0] - 1], row_ref[...], col_ref[...])

    scores = mm_last(q_ref[0], k_ref[0]) * (SCALE * LOG2_E) + bias_ref[...]
    powers = jnp.exp2(scores - jnp.max(scores, axis=-1, keepdims=True))
    weights = powers * (1.0 / jnp.sum(powers, axis=-1, keepdims=True))
    o_ref[...] = to_low(mm(to_low(weights), v_ref[0]))


def attend(q, k, v, place, where, block=256):
    heads, n, hd = q.shape
    whole = pl.BlockSpec((1, n, hd), lambda b, t, w: (t, 0, 0))
    return pl.pallas_call(
        attend_kernel,
        out_shape=jax.ShapeDtypeStruct((n, heads * hd), BF16),
        grid_spec=pltpu.PrefetchScalarGridSpec(
            num_scalar_prefetch=1,
            grid=(n // block, heads),
            in_specs=[
                pl.BlockSpec((1, block, hd), lambda b, t, w: (t, b, 0)),
                whole,
                whole,
                pl.BlockSpec((block, 1), lambda b, t, w: (b, 0)),
                pl.BlockSpec((1, n), lambda b, t, w: (0, 0)),
            ],
            out_specs=pl.BlockSpec((block, hd), lambda b, t, w: (b, w[t])),
            scratch_shapes=[pltpu.VMEM((block, n), F32)],
        ),
        compiler_params=pltpu.CompilerParams(vmem_limit_bytes=VMEM),
        cost_estimate=pl.CostEstimate(
            flops=4 * heads * n * n * hd, bytes_accessed=8 * heads * n * hd, transcendentals=heads * n * n
        ),
        name="attend",
    )(where, q, k, v, place[:, None], place[None, :])


def attend_back_kernel(where_ref, q_ref, k_ref, v_ref, do_ref, row_ref, col_ref, dq_ref, dk_ref, dv_ref, products_ref, bias_ref):
    t, b = pl.program_id(0), pl.program_id(1)

    @pl.when(pl.program_id(0) == 0)
    def _():
        bias_ref[b] = bias_of(where_ref[where_ref.shape[0] - 1], row_ref[...], col_ref[...])

    q, k, v, do = q_ref[0], k_ref[0], v_ref[0], do_ref[...]
    scores = mm_last(k, q) * (SCALE * LOG2_E) + bias_ref[b]
    powers = jnp.exp2(scores - jnp.max(scores, axis=0, keepdims=True))
    probs = powers * (1.0 / jnp.sum(powers, axis=0, keepdims=True))
    grad_probs = mm_last(v, do)
    delta = jnp.sum(probs * grad_probs, axis=0, keepdims=True)
    grad_scores = to_low(probs * (grad_probs - delta))
    dq = mm_first(grad_scores, k) * SCALE
    dq_ref[0] = dq
    dk = mm(grad_scores, q) * SCALE
    dv = mm(to_low(probs), do)

    @pl.when((t == 0) & (b == 0))
    def _():
        products_ref[...] = jnp.zeros_like(products_ref)

    own = pl.ds(pl.multiple_of(b * q.shape[0], q.shape[0]), q.shape[0])
    products_ref[0:1, own] += jnp.sum((dq * q.astype(F32)).T, axis=0, keepdims=True)

    @pl.when(b == 0)
    def _():
        dk_ref[0] = dk
        dv_ref[0] = dv

    @pl.when(b > 0)
    def _():
        dk_ref[0] += dk
        dv_ref[0] += dv

    @pl.when(b == pl.num_programs(1) - 1)
    def _():
        products_ref[1:2, :] += jnp.sum((dk_ref[0] * k.astype(F32)).T, axis=0, keepdims=True)


def attend_back(q, k, v, do, place, where, block=512):
    heads, n, hd = q.shape
    one = pl.BlockSpec((1, block, hd), lambda t, b, w: (t, b, 0))
    whole = pl.BlockSpec((1, n, hd), lambda t, b, w: (t, 0, 0))
    return pl.pallas_call(
        attend_back_kernel,
        out_shape=[jax.ShapeDtypeStruct((heads, n, hd), F32)] * 3 + [jax.ShapeDtypeStruct((2, n), F32)],
        grid_spec=pltpu.PrefetchScalarGridSpec(
            num_scalar_prefetch=1,
            grid=(heads, n // block),
            in_specs=[
                one,
                whole,
                whole,
                pl.BlockSpec((block, hd), lambda t, b, w: (b, w[t])),
                pl.BlockSpec((1, block), lambda t, b, w: (0, b)),
                pl.BlockSpec((n, 1), lambda t, b, w: (0, 0)),
            ],
            out_specs=[one, whole, whole, pl.BlockSpec((2, n), lambda t, b, w: (0, 0))],
            scratch_shapes=[pltpu.VMEM((n // block, n, block), F32)],
        ),
        compiler_params=pltpu.CompilerParams(vmem_limit_bytes=32 << 20),
        cost_estimate=pl.CostEstimate(
            flops=10 * heads * n * n * hd, bytes_accessed=20 * heads * n * hd, transcendentals=heads * n * n
        ),
        name="attend_back",
    )(where, q, k, v, do, place[None, :], place[:, None])


def columns_of(t, i):
    return slice((3 * t + i) * HEAD_DIM, (3 * t + i + 1) * HEAD_DIM)


def squares_kernel(heads, raw_ref, out_ref):
    for i in (0, 1):
        total = sum(jnp.square(raw_ref[:, columns_of(t, i)]) for t in range(heads))
        out_ref[i : i + 1, :] = jnp.sum(total.T, axis=0, keepdims=True)


def squares(raw, heads, block=256):
    n, width = raw.shape
    return pl.pallas_call(
        lambda *refs: squares_kernel(heads, *refs),
        out_shape=jax.ShapeDtypeStruct((2, n), F32),
        grid=(n // block,),
        in_specs=[pl.BlockSpec((block, width), lambda b: (b, 0))],
        out_specs=pl.BlockSpec((2, block), lambda b: (0, b)),
        compiler_params=pltpu.CompilerParams(vmem_limit_bytes=VMEM),
        cost_estimate=pl.CostEstimate(flops=heads * n * 512, bytes_accessed=heads * n * 1536, transcendentals=0),
        name="squares",
    )(raw)


def turn_half(tensor):
    return pltpu.roll(tensor, HEAD_DIM // 2, 1)


def rope_kernel(heads, raw_ref, inv_ref, gain_ref, turn_ref, q_ref, k_ref, v_ref):
    cosines, sines = turn_ref[:, :HEAD_DIM], turn_ref[:, HEAD_DIM:]
    for t in range(heads):
        for i, out in enumerate((q_ref, k_ref)):
            value = raw_ref[:, columns_of(t, i)] * inv_ref[:, i : i + 1] * gain_ref[t, i : i + 1, :]
            out[t] = to_low(value * cosines + turn_half(value) * sines)
        v_ref[t] = to_low(raw_ref[:, columns_of(t, 2)])


def rope(raw, inv, gain, turn, block=256):
    heads, n = gain.shape[0], raw.shape[0]
    rows = lambda width: pl.BlockSpec((block, width), lambda b: (b, 0))
    out = pl.BlockSpec((heads, block, HEAD_DIM), lambda b: (0, b, 0))
    return pl.pallas_call(
        lambda *refs: rope_kernel(heads, *refs),
        out_shape=[jax.ShapeDtypeStruct((heads, n, HEAD_DIM), BF16)] * 3,
        grid=(n // block,),
        in_specs=[
            rows(raw.shape[1]),
            rows(2),
            pl.BlockSpec((heads, 2, HEAD_DIM), lambda b: (0, 0, 0)),
            rows(2 * HEAD_DIM),
        ],
        out_specs=[out] * 3,
        compiler_params=pltpu.CompilerParams(vmem_limit_bytes=VMEM),
        cost_estimate=pl.CostEstimate(flops=heads * n * 2000, bytes_accessed=heads * n * 2304, transcendentals=0),
        name="rope",
    )(raw, inv, gain, turn)


def rope_back_kernel(
    heads, raw_ref, dq_ref, dk_ref, dv_ref, inv_ref, mean_ref, gain_ref, turn_ref, out_ref, grad_ref
):
    @pl.when(pl.program_id(0) == 0)
    def _():
        grad_ref[...] = jnp.zeros_like(grad_ref)

    cosines, sines = turn_ref[:, :HEAD_DIM], turn_ref[:, HEAD_DIM:]
    for t in range(heads):
        for i, grad in enumerate((dq_ref, dk_ref)):
            inv = inv_ref[:, i : i + 1]
            hat = raw_ref[:, columns_of(t, i)] * inv
            back = grad[t] * cosines - turn_half(grad[t]) * sines
            grad_ref[t, i : i + 1, :] += jnp.sum(back * hat, axis=0, keepdims=True)
            row = inv * (back * gain_ref[t, i : i + 1, :] - hat * mean_ref[:, i : i + 1])
            out_ref[:, columns_of(t, i)] = to_low(row)
        out_ref[:, columns_of(t, 2)] = to_low(dv_ref[t])


def rope_back(raw, dq, dk, dv, inv, mean, gain, turn, block=256):
    heads, (n, width) = gain.shape[0], raw.shape
    rows = lambda width: pl.BlockSpec((block, width), lambda b: (b, 0))
    grad = pl.BlockSpec((heads, block, HEAD_DIM), lambda b: (0, b, 0))
    gains = pl.BlockSpec((heads, 2, HEAD_DIM), lambda b: (0, 0, 0))
    return pl.pallas_call(
        lambda *refs: rope_back_kernel(heads, *refs),
        out_shape=[jax.ShapeDtypeStruct((n, width), BF16), jax.ShapeDtypeStruct((heads, 2, HEAD_DIM), F32)],
        grid=(n // block,),
        in_specs=[rows(width)] + [grad] * 3 + [rows(2), rows(2), gains, rows(2 * HEAD_DIM)],
        out_specs=[rows(width), gains],
        compiler_params=pltpu.CompilerParams(vmem_limit_bytes=WIDE_VMEM),
        cost_estimate=pl.CostEstimate(flops=heads * n * 4000, bytes_accessed=heads * n * 3840, transcendentals=0),
        name="rope_back",
    )(raw, dq, dk, dv, inv, mean, gain, turn)


def body(
    tokens,
    piece_start,
    positions,
    w_query,
    w_key,
    w_value,
    w_out,
    query_gain,
    key_gain,
    attn_gain,
    w_gate,
    w_up,
    w_down,
    mlp_gain,
    cotangent,
):
    S = lax.axis_size("shard")
    R = lax.axis_size("rep")
    s = lax.axis_index("shard")
    r = lax.axis_index("rep")
    _, span, width = tokens.shape
    heads = HEADS // S
    per = HEADS // R
    own_width = width // S
    x_own = tokens.reshape(span, width)

    by_ring = per * 2 == S
    chip, core = r // 2, r % 2

    def head_columns(j):
        start = j * HEAD_DIM
        return jnp.concatenate(
            [to_low(lax.dynamic_slice_in_dim(w, start, HEAD_DIM, 1)) for w in (w_query, w_key, w_value)], axis=1
        )

    def by_core(value):
        if not by_ring:
            return value
        middle = value.shape[1] // 2
        return jnp.where(core == 1, jnp.concatenate([value[:, middle:], value[:, :middle]], axis=1), value)

    own_columns = [head_columns((s + k) % per) for k in range(per)]
    got = [permute(value, heads_perm(S, R, per, k)) for k, value in enumerate(own_columns)]
    gains_own = jnp.stack([to_low(g).astype(F32) for g in (query_gain, key_gain, attn_gain, mlp_gain)])
    small = jnp.concatenate([positions.reshape(span).astype(F32), gains_own.reshape(-1)])
    small_all = [small] + [send_shard(small, k) for k in range(1, S)]
    own_out = spread_heads(after(to_low(w_out), *own_columns).reshape(heads, HEAD_DIM, -1), s)
    got, small_all, own_out = lax.optimization_barrier((got, small_all, own_out))

    got = reverse_pick(jnp.stack(got), s % per).reshape(per * own_width, 3 * HEAD_DIM)
    if by_ring:
        qkv_pairs = gather_pairs(got, R)
        qkv_w = jnp.zeros((width, heads * 3 * HEAD_DIM), BF16)
        for t, pair in enumerate(qkv_pairs):
            for i, block in enumerate(pair):
                qkv_w = lax.dynamic_update_slice(qkv_w, block, (i * block.shape[0], t * block.shape[1]))
        head_order = (chip - jnp.arange(heads)) % heads
        ring_start, ring_late, ring_end = qkv_pairs[1][0], qkv_pairs[-2][0], qkv_pairs[-1][0]
    else:
        qkv_w = lax.all_gather(got, "rep", axis=0, tiled=True).reshape(heads, width, 3 * HEAD_DIM)
        qkv_w = jnp.concatenate(list(qkv_w), axis=1)
        head_order = jnp.arange(heads)
        ring_start = ring_late = ring_end = qkv_w
    where = jnp.concatenate([head_order, piece_start]).astype(jnp.int32)
    x_all, x_last = gather_tokens(by_core(after(x_own, got)), (ring_start,), (ring_late,))
    gate_up = after(jnp.concatenate([to_low(w_gate), to_low(w_up)], axis=1), x_last)
    gate_up_w = lax.all_gather(gate_up, "shard", axis=0, tiled=True)

    own_out = own_out.reshape(own_width, -1)
    columns = own_out.shape[1]

    gains = unrelative(jnp.stack([v[span:].reshape(4, own_width) for v in small_all]), s)
    gains = gains.transpose(1, 0, 2).reshape(4, width)
    head_gains = gains[:2].reshape(2, heads, S, HEAD_DIM)
    head_gains = lax.dynamic_index_in_dim(head_gains, s, 2, keepdims=False)
    head_gains = head_gains.transpose(1, 0, 2)
    if by_ring:
        head_gains = reverse_pick(head_gains, chip)
    again, mgain = gains[2], gains[3]
    order = token_order(S)
    step = S * span // len(order)
    place_pos = jnp.concatenate([small_all[j][h * step : (h + 1) * step] for h, j in order])
    place = jnp.concatenate([(s ^ j) * span + h * step + lax.iota(jnp.int32, step) for h, j in order])
    angles = place_pos[:, None] * frequencies()
    cosines, sines = jnp.cos(angles), jnp.sin(angles)
    turn = jnp.concatenate([cosines, cosines, -sines, sines], axis=1)

    raw = mm(x_all, qkv_w)
    raw_squares = squares(raw, heads)
    inv = lax.rsqrt(sum_rows(raw_squares) / width + epsilon).T
    q, k, v = rope(raw, inv, head_gains, turn)
    pieces = spread_down(after(to_low(w_down), q))
    o = attend(q, k, v, place, where)

    out_w = jnp.zeros((own_width, width), BF16)
    block = after(own_out, ring_end)
    for t in range(R // 2):
        if t:
            block = after(ring(block, R), (raw_squares, q, o)[min(t - 1, 2)])
        for i, value in enumerate((block, sibling(block, R))):
            start = ((chip - t) % (R // 2) * 2 + (core ^ i)) * columns
            out_w = lax.dynamic_update_slice_in_dim(out_w, value, start, 1)
    rows = S * span // 2
    a_send = mm(o[rows:], out_w)
    a_keep = mm(after(o[:rows], to_low(a_send)), out_w)
    down_blocks = exchange(after(pieces, a_keep), "rep")
    a = scatter_tokens(a_keep, a_send, (down_blocks,))
    ainv = lax.rsqrt(jnp.mean(a * a, axis=-1, keepdims=True) + epsilon)
    ahat = a * ainv
    h = x_own.astype(F32) + ahat * again
    hb = to_low(h)

    down_w = lax.all_gather(join_down(after(down_blocks, hb)), "shard", axis=0, tiled=True)
    chips, ff = R // 2, w_gate.shape[1]
    kept = {}

    def forward(t, pair):
        gu = mm(pair, gate_up_w)
        g, u = gu[:, :ff], gu[:, ff:]
        inner = to_low(g * jax.nn.sigmoid(g) * u)
        kept[t] = (g, u, inner, pair)
        return mm(inner, down_w)

    z = round_the_ring(hb, forward, R, lambda t: (), lambda step, low: (), True)
    zinv = lax.rsqrt(jnp.mean(z * z, axis=-1, keepdims=True) + epsilon)
    zhat = z * zinv
    output = to_low(h + zhat * mgain).reshape(tokens.shape)

    dy = cotangent.reshape(span, width).astype(F32)
    grad_mgain = jnp.sum(dy * zhat, axis=0)
    scaled = dy * mgain
    dz = to_low(zinv * (scaled - zhat * jnp.mean(scaled * zhat, axis=-1, keepdims=True)))
    dgs, dus, dz_pairs, dh_parts, weight_grads = {}, {}, {}, {}, {}

    def backward(t, pair):
        g, u = kept[t][:2]
        dm = mm_last(pair, down_w)
        sig = jax.nn.sigmoid(g)
        dz_pairs[t] = pair
        dgs[t] = to_low(dm * u * sig * (1.0 + g * (1.0 - sig)))
        dus[t] = to_low(dm * g * sig)
        dh_parts[t] = mm_last(jnp.concatenate([dgs[t], dus[t]], axis=1), gate_up_w)
        return dh_parts[t]

    def all_tokens(values, hold):
        return jnp.concatenate([after(values[t], hold) for t in range(chips)])

    def weight_grad(step, low):
        hold = (dh_parts[chips - 1],) if step == 0 else ()
        if step == chips - 3:
            inner_all = all_tokens({t: kept[t][2] for t in kept}, low)
            down_grad = to_low(mm_first(inner_all, all_tokens(dz_pairs, low)))
            weight_grads["down"] = down_grad
            weight_grads["down_share"] = lax.psum_scatter(down_grad, "shard", scatter_dimension=0, tiled=True)
            hold += (down_grad,)
        if step == chips - 2:
            hb_all = all_tokens({t: kept[t][3] for t in kept}, low)
            weight_grads["gate"] = to_low(mm_first(hb_all, all_tokens(dgs, low)))
            weight_grads["up"] = to_low(mm_first(hb_all, all_tokens(dus, low)))
            hold += (weight_grads["gate"],)
        return hold

    dh = dy + round_the_ring(dz, backward, R, lambda t: (dh_parts[t],), weight_grad)

    grad_again = jnp.sum(dh * ahat, axis=0)
    scaled = dh * again
    da = to_low(ainv * (scaled - ahat * jnp.mean(scaled * ahat, axis=-1, keepdims=True)))
    gate_up_grad = jnp.concatenate([weight_grads["gate"], after(weight_grads["up"], da)], axis=1)
    da_all, _ = gather_tokens(da, (), (gate_up_grad, weight_grads["down_share"]))
    do = to_low(mm_last(da_all, out_w))
    gate_up_share = lax.psum_scatter(after(gate_up_grad, da_all), "shard", scatter_dimension=0, tiled=True)
    dq, dk, dv, products = attend_back(q, k, v, do, place, where)
    down_back = after(exchange(part_down(after(weight_grads["down_share"], da_all)), "rep"), dv)
    products = after(products, down_back)
    means = (sum_rows(products) / width).T
    dqkv, head_grads = rope_back(raw, dq, dk, dv, inv, means, head_gains, turn)
    if by_ring:
        head_grads = reverse_pick(head_grads, chip)
    grad_down = collect_down(down_back)
    dqkv = after(dqkv, grad_down)
    grad_down = grad_down.astype(F32)
    late = {}
    qkv_grad = to_low(mm_first(x_all, dqkv))

    def qkv_part(t, hold):
        return qkv_grad[:, t * 3 * HEAD_DIM : (t + 1) * 3 * HEAD_DIM]

    def input_grad(i, hold=None):
        if i == 0:
            dx_all = mm_last(after(dqkv, hold), qkv_w)
            late["keep"], late["send"] = dx_all[:rows], to_low(dx_all[rows:])
            out_grad = to_low(mm_first(o, after(da_all, hold)))
            late["out"] = lax.psum_scatter(out_grad, "rep", scatter_dimension=1, tiled=True)
            late["gains"] = gain_shares(after(head_grads, hold), s)
            return (late["keep"], late["send"], late["gains"], gate_up_share, out_grad)
        if i == 2:
            late["hold"] = (hold,)
            late["out"] = collect_heads(after(late["out"], hold).reshape(heads, HEAD_DIM, -1), s)
            return (late["out"],)
        return ()

    def gain_shares(head_grads, s):
        wide = jnp.stack([grad_again, grad_mgain]).reshape(2, S, own_width).transpose(1, 0, 2)
        if heads != S:
            head_grads = collect_heads(head_grads, s)
            wide = jnp.sum(exchange(wide, "shard"), axis=0)
        else:
            got = exchange(jnp.concatenate([head_grads, wide], axis=2), "shard")
            head_grads, wide = got[..., :HEAD_DIM], jnp.sum(got[..., HEAD_DIM:], axis=0)
        return jnp.concatenate([head_grads.transpose(1, 0, 2).reshape(2, own_width), wide])

    if by_ring:
        qkv_share = to_low(scatter_pairs(qkv_part, R, input_grad))
    else:
        parts = jnp.concatenate([qkv_part(t, None) for t in range(heads)])
        qkv_share = lax.psum_scatter(parts, "rep", scatter_dimension=0, tiled=True)
        input_grad(0, dqkv)
    dx = dh + by_core(scatter_tokens(late["keep"], late["send"], late.get("hold", ()), (qkv_share,)))

    if not by_ring:
        late["out"] = collect_heads(late["out"].reshape(heads, HEAD_DIM, -1), s)
    grad_out = late["out"].reshape(w_out.shape).astype(F32)
    slots = qkv_share.reshape(per, own_width, 3 * HEAD_DIM)
    back = jnp.stack([permute(pick(slots, (s - k) % per), flip(heads_perm(S, R, per, k))) for k in range(per)])
    back = roll_pick(back, -(s % per)).reshape(per, own_width, 3, HEAD_DIM)
    back = back.transpose(2, 1, 0, 3).reshape(3, own_width, per * HEAD_DIM).astype(F32)

    gain_grads = sum_rep(after(late["gains"], qkv_share))
    gate_up_share = gate_up_share.astype(F32)

    return (
        output,
        dx.reshape(tokens.shape),
        back[0],
        back[1],
        back[2],
        grad_out,
        gain_grads[0],
        gain_grads[1],
        gain_grads[2],
        gate_up_share[:, :ff],
        gate_up_share[:, ff:],
        grad_down,
        gain_grads[3],
    )


def solution(mesh):
    grid = P("shard", "rep")
    rows = P("rep", "shard", None)
    gain = P("shard")
    in_specs = (rows, P("rep"), P("rep", "shard"), grid, grid, grid, grid, gain, gain, gain, grid, grid, grid, gain, rows)
    out_specs = (rows, rows, grid, grid, grid, grid, gain, gain, gain, grid, grid, grid, gain)
    return jax.shard_map(body, mesh=mesh, in_specs=in_specs, out_specs=out_specs, check_vma=False)
```
